32 devices in a mesh: group: 2 (over y), col: 8 (over z, x), row: 2 (over core).
Axes of the slice: x: 2, y: 2, z: 4, core: 2. Of those that a mesh axis runs over, the one named last changes fastest.
Arguments:
- tile_values: bfloat16 [768, 256, 256], P(('group', 'col', 'row')), parts along dimension 0, may hold values from -0.75 to 0.75
- tile_blocks: int32 [768, 2], P(('group', 'col', 'row')), parts along dimension 0, may hold values from 0 to 511, as said below
- scale_index: int32 [768], P(('group', 'col', 'row')), parts along dimension 0, may hold values from 0 to 15
- scale_table: float32 [32], P('group'), parts along dimension 0, may hold values from 0.5 to 2
- primal_iter: float32 [16, 16384], P(('group', 'col'), 'row'), parts along dimension 0, may hold values from -6 to 6
- dual_iter: float32 [4, 8192], P(('group', 'row'), 'col'), parts along dimension 0, may hold values from -0.36 to 0.36
- objective: float32 [16, 16384], P(('group', 'col'), 'row'), parts along dimension 0, may hold values from -0.3 to 0.3
- right_side: float32 [4, 8192], P(('group', 'row'), 'col'), parts along dimension 0, may hold values from -6 to 6
- lower_bound: float32 [16, 16384], P(('group', 'col'), 'row'), parts along dimension 0, may hold values from -1.2 to 0.95, as said below
- upper_bound: float32 [16, 16384], P(('group', 'col'), 'row'), parts along dimension 0, may hold values from -0.95 to 1.2, as said below
- bound_kind: int32 [16, 16384], P(('group', 'col'), 'row'), parts along dimension 0, may hold values from 0 to 3
- row_kind: int32 [4, 8192], P(('group', 'row'), 'col'), parts along dimension 0, may hold values from 0 to 1
- step_sizes: float32 [4], P('group'), parts along dimension 0, may hold values from 0.2 to 0.8
Outputs:
- primal_next: float32 [16, 16384], P(('group', 'col'), 'row'), parts along dimension 0
- dual_next: float32 [4, 8192], P(('group', 'row'), 'col'), parts along dimension 0
- restart_stats: float32 [6], P('group'), parts along dimension 0
The draws below stay inside these ranges and needn't reach their ends.
There are 2 independent parts, one for each index of `group`. The reference program is written for one: setup_inputs(seed, part) draws one part's arguments, and reference() takes and returns one part's arrays. A program takes and returns all parts, laid end to end along the dimension named above; each array names one. Nothing has to cross between parts.
Inputs may be any that keep to these rules, and one draw needn't show every extreme that they name: tile_blocks[s, 0] is a row block and tile_blocks[s, 1] a column block. With s a tile's index within its part, g = s // 24, c = g // 2 and r = g % 2, the row block lies in r * 32 to (r + 1) * 32 - 1 and the column block in c * 64 to (c + 1) * 64 - 1. Write o = (row block - r * 32) * 256 // 1024 for the col index whose rows hold a tile's row block: among the 24 tiles of one g, at most 3 share one o, and exactly 3 share some o. lower_bound is below upper_bound in every entry. upper_bound is above lower_bound in every entry.
All inputs are finite; a program needn't handle non-finite values.
Results may differ from the reference program's by a relative error of at most 0.0003.
The reference program's roundings to bfloat16 on the way count: a program that leaves them out, or rounds other values in their place, can miss the bound.
Values may be sent and summed in bfloat16 or wider, within the bound.
A program may use at most 64 MiB of HBM per device.

```python
import math
import jax
import jax.numpy as jnp
from jax import lax

TB = 256
NSCALE = 16
COLS_DEV = 8192
ROWS_DEV = 1024
TILES_PER_DEVICE = 24
CSEGS = 8
RSEGS = 2
CSEG_LEN = 16384
RSEG_LEN = 8192
NCOLS = 131072
NROWS = 16384
TILES = 384
N_COL = 8
N_ROW = 2


def box_parts(key):
    shared = jax.random.fold_in(key, 21)
    key_center, key_half = jax.random.split(shared)
    shape = (CSEGS, CSEG_LEN)
    centers = jax.random.uniform(key_center, shape, jnp.float32, -1.0, 1.0)
    halves = jax.random.uniform(key_half, shape, jnp.float32, 0.05, 0.2)
    return (centers, halves)


def draw_lower_bound(key, part):
    centers, halves = box_parts(key)
    return (centers - halves).astype(jnp.float32)


def draw_upper_bound(key, part):
    centers, halves = box_parts(key)
    return (centers + halves).astype(jnp.float32)


def draw_tile_blocks(key, part):
    key = jax.random.fold_in(key, 7)
    key_rows, key_cols, key_owner = jax.random.split(key, 3)
    devices_part = N_COL * N_ROW
    total_tiles = TILES_PER_DEVICE * devices_part
    position = jnp.arange(total_tiles, dtype=jnp.int32)
    device = position // TILES_PER_DEVICE
    within_dev = position % TILES_PER_DEVICE
    col_seg = device // N_ROW
    row_seg = device % N_ROW
    row_span = ROWS_DEV * N_COL // TB
    col_span = COLS_DEV * N_ROW // TB
    per_owner = ROWS_DEV // TB
    owner_keys = jax.random.split(key_owner, devices_part)
    orders = jax.vmap(lambda one: jax.random.permutation(one, N_COL))(owner_keys).astype(jnp.int32)
    owners = orders[device, within_dev % N_COL]
    rows = row_seg * row_span + owners * per_owner + jax.random.randint(key_rows, (total_tiles,), 0, per_owner)
    cols = col_seg * col_span + jax.random.randint(key_cols, (total_tiles,), 0, col_span)
    cols = jnp.where(position == 0, 0, jnp.where(position == total_tiles - 1, col_span * N_COL - 1, cols))
    return jnp.stack([rows, cols], axis=1).astype(jnp.int32)


def set_ends(array, key, low, top_value):
    longest = array.shape.index(max(array.shape))
    spots = []
    for shift in (0, 1):
        where = [jax.random.randint(jax.random.fold_in(key, axis), (), 0, length) for axis, length in enumerate(array.shape)]
        where[longest] = (where[longest] + shift) % array.shape[longest]
        spots.append(tuple(where))
    return array.at[spots[0]].set(low).at[spots[1]].set(top_value)


def levels(stream_key, dims, shards, low, largest):
    loudness, own = 1.0, jax.random.fold_in(stream_key, 6)
    for axis_at, parts in shards:
        steps = jnp.exp(jax.random.uniform(jax.random.fold_in(own, axis_at), (parts,), jnp.float32, low / len(shards), largest / len(shards)))
        loudness = loudness * jnp.repeat(steps, dims[axis_at] // parts).reshape([-1 if axis == axis_at else 1 for axis in range(len(dims))])
    return loudness


def scatter_about(stream_key, shape, width, limit, cuts=(), kind=jnp.bfloat16):
    result = width * jax.random.normal(stream_key, shape, jnp.float32)
    if cuts:
        result = result * levels(stream_key, shape, cuts, -0.22, 0.18)
    return jnp.clip(result, -limit, limit).astype(kind)


def setup_inputs(seed: int = 0, part: int = 0) -> dict:
    key_of = jax.random.split(jax.random.key(seed), 14)
    own_keys = jax.random.split(jax.random.fold_in(key_of[13], part), 14)
    tile_values = scatter_about(own_keys[0], (TILES, TB, TB), (TB // 4) ** -0.5, 0.75, ((0, 16),))
    tile_blocks = draw_tile_blocks(jax.random.fold_in(jax.random.fold_in(key_of[13], part), 71), part)
    scale_index = set_ends(jax.random.randint(own_keys[2], (TILES,), 0, NSCALE), jax.random.fold_in(own_keys[2], 1), 0, NSCALE - 1).astype(jnp.int32)
    scale_table = jnp.clip(jnp.exp(jax.random.uniform(own_keys[3], (NSCALE,), jnp.float32, math.log(0.5), math.log(2.0))), 0.5, 2.0)
    primal_iter = scatter_about(own_keys[4], (CSEGS, CSEG_LEN), 1.0, 6.0, ((0, 8), (1, 2)), jnp.float32)
    dual_iter = scatter_about(own_keys[5], (RSEGS, RSEG_LEN), 0.06, 0.36, ((0, 2), (1, 8)), jnp.float32)
    objective = scatter_about(own_keys[6], (CSEGS, CSEG_LEN), 0.05, 0.3, ((0, 8), (1, 2)), jnp.float32)
    right_side = scatter_about(own_keys[7], (RSEGS, RSEG_LEN), 1.0, 6.0, ((0, 2), (1, 8)), jnp.float32)
    lower_bound = draw_lower_bound(jax.random.fold_in(jax.random.fold_in(key_of[13], part), 71), part)
    upper_bound = draw_upper_bound(jax.random.fold_in(jax.random.fold_in(key_of[13], part), 71), part)
    bound_kind = set_ends(jax.random.randint(own_keys[10], (CSEGS, CSEG_LEN), 0, 4), jax.random.fold_in(own_keys[10], 1), 0, 3).astype(jnp.int32)
    row_kind = set_ends(jax.random.randint(own_keys[11], (RSEGS, RSEG_LEN), 0, 2), jax.random.fold_in(own_keys[11], 1), 0, 1).astype(jnp.int32)
    step_sizes = jnp.clip(jax.random.uniform(own_keys[12], (2,), jnp.float32, 0.2, 0.8), 0.2, 0.8)
    return {"tile_values": tile_values, "tile_blocks": tile_blocks, "scale_index": scale_index, "scale_table": scale_table, "primal_iter": primal_iter, "dual_iter": dual_iter, "objective": objective, "right_side": right_side, "lower_bound": lower_bound, "upper_bound": upper_bound, "bound_kind": bound_kind, "row_kind": row_kind, "step_sizes": step_sizes}


def reference(tile_values, tile_blocks, scale_index, scale_table, primal_iter, dual_iter, objective, right_side, lower_bound, upper_bound, bound_kind, row_kind, step_sizes):
    groups = TILES // TILES_PER_DEVICE
    scales = scale_table[scale_index]
    values_g = tile_values.reshape(groups, TILES_PER_DEVICE, TB, TB)
    blocks_g = tile_blocks.reshape(groups, TILES_PER_DEVICE, 2)
    scales_g = scales.reshape(groups, TILES_PER_DEVICE)
    x_vec = primal_iter.reshape(NCOLS)
    y_vec = dual_iter.reshape(NROWS)
    c_vec = objective.reshape(NCOLS)
    b_vec = right_side.reshape(NROWS)
    low_vec = lower_bound.reshape(NCOLS)
    up_vec = upper_bound.reshape(NCOLS)
    kinds = bound_kind.reshape(NCOLS)
    row_kinds = row_kind.reshape(NROWS)
    y_blocks = dual_iter.astype(jnp.bfloat16).reshape(NROWS // TB, TB)

    def transposed(total, group):
        entry_values, blocks, scale_factor = group
        selected_entries = y_blocks[blocks[:, 0]].astype(jnp.float32)
        single_term = jnp.einsum('stk,st->sk', entry_values.astype(jnp.float32), selected_entries) * scale_factor[:, None]
        return (total.at[blocks[:, 1]].add(single_term), None)
    aty, _ = lax.scan(transposed, jnp.zeros((NCOLS // TB, TB), jnp.float32), (values_g, blocks_g, scales_g))
    reduced = c_vec - aty.reshape(NCOLS)
    has_low = (kinds == 1) | (kinds == 3)
    has_up = (kinds == 2) | (kinds == 3)
    moved = x_vec - step_sizes[0] * reduced
    moved = jnp.where(has_low, jnp.maximum(moved, low_vec), moved)
    x_next = jnp.where(has_up, jnp.minimum(moved, up_vec), moved)
    zero = jnp.zeros_like(reduced)
    dual_resid = jnp.where(kinds == 0, reduced, jnp.where(kinds == 1, jnp.minimum(reduced, 0.0), jnp.where(kinds == 2, jnp.maximum(reduced, 0.0), zero)))
    bound_terms = jnp.where(has_low, low_vec * jnp.maximum(reduced, 0.0), zero) + jnp.where(has_up, up_vec * jnp.minimum(reduced, 0.0), zero)
    gap = jnp.sum(c_vec * x_next) - jnp.sum(b_vec * y_vec) - jnp.sum(bound_terms)
    pair_b = jnp.stack([2.0 * x_next - x_vec, x_next]).astype(jnp.bfloat16).reshape(2, NCOLS // TB, TB)

    def forward(total, group):
        entry_values, blocks, scale_factor = group
        selected_entries = pair_b[:, blocks[:, 1]].astype(jnp.float32)
        single_term = jnp.einsum('ixj,pij->pix', entry_values.astype(jnp.float32), selected_entries) * scale_factor[None, :, None]
        return (total.at[:, blocks[:, 0]].add(single_term), None)
    axs, _ = lax.scan(forward, jnp.zeros((2, NROWS // TB, TB), jnp.float32), (values_g, blocks_g, scales_g))
    axs = axs.reshape(2, NROWS)
    ineq = row_kinds == 1
    y_next = y_vec + step_sizes[1] * (b_vec - axs[0])
    y_next = jnp.where(ineq, jnp.maximum(y_next, 0.0), y_next)
    primal_resid = b_vec - axs[1]
    primal_resid = jnp.where(ineq, jnp.maximum(primal_resid, 0.0), primal_resid)
    stats = jnp.stack([jnp.sum(primal_resid * primal_resid) / NROWS, jnp.sum(dual_resid * dual_resid) / NCOLS, gap / math.sqrt(NCOLS)])
    return (x_next.reshape(CSEGS, CSEG_LEN), y_next.reshape(RSEGS, RSEG_LEN), stats)
```

```python
import functools
import math

import jax
import jax.numpy as jnp
from jax import lax
from jax.experimental import pallas as pl
from jax.experimental.pallas import tpu as pltpu
from jax.sharding import PartitionSpec as P

F32 = jnp.float32
BF16 = jnp.bfloat16
MESH = pl.DeviceIdType.MESH
LANES = 128


def each(count, body):
    if count <= 17:
        for k in range(1, count):
            body(k)
    else:
        lax.fori_loop(1, count, lambda k, _: (body(k), 0)[1], 0)


def three_parts(v):
    hi = v.astype(BF16)
    rest = v - hi.astype(F32)
    mid = rest.astype(BF16)
    low = (rest - mid.astype(F32)).astype(BF16)
    return hi, mid, low


def iota(shape, dim):
    return lax.broadcasted_iota(jnp.int32, shape, dim)


def kernel(
    n_col,
    n_row,
    tv, tb, si, st, x_h, y_h, c_h, b_h, l_h, u_h, k_h, e_h, step,
    xn_o, yn_o, stat_o,
    tiles, prim, kind, ybuf, bbuf, ebuf, meta, part, xn_s, yn_s, terms, rt, sbuf,
    lsem, ysend, yrecv, rsend, rrecv, tsend, trecv, ssend, srecv,
):
    count, size, _ = tv.shape
    groups = count // 8
    cblocks = prim.shape[2]
    n_dev = n_col * n_row
    col = lax.axis_index("col")
    row = lax.axis_index("row")
    other = 1 - row
    dev = col * n_row + row
    row_span = ybuf.shape[1] // 2 * n_col
    col_span = cblocks

    y_in = pltpu.make_async_copy(y_h, ybuf.at[col], lsem.at[0])
    y_in.start()

    barrier = pltpu.get_barrier_semaphore()

    def greet(k):
        q = lax.rem(dev + k, n_dev)
        pl.semaphore_signal(
            barrier,
            inc=1,
            device_id={"col": lax.div(q, n_row), "row": lax.rem(q, n_row)},
            device_id_type=MESH,
        )

    each(n_dev, greet)

    chunk = count // 4
    tile_in = []
    for i in range(4):
        span = pl.ds(i * chunk, chunk)
        copy = pltpu.make_async_copy(tv.at[span], tiles.at[span], lsem.at[1 + i])
        copy.start()
        tile_in.append(copy)
    small_in = [
        pltpu.make_async_copy(src, prim.at[i, row], lsem.at[5 + i])
        for i, src in enumerate((x_h, c_h, l_h, u_h))
    ]
    small_in.append(pltpu.make_async_copy(k_h, kind.at[row], lsem.at[9]))
    small_in.append(pltpu.make_async_copy(b_h, bbuf, lsem.at[10]))
    small_in.append(pltpu.make_async_copy(e_h, ebuf, lsem.at[11]))
    for copy in small_in:
        copy.start()

    sub8 = iota((8, LANES), 0)
    lane8 = iota((8, LANES), 1)
    lane256 = iota((8, 2 * LANES), 1)
    rows_l = [tb[0, s] - row * row_span for s in range(count)]
    cols_l = [tb[1, s] - col * col_span for s in range(count)]
    own = lane8 // 64 == row
    spot = lane8 % 64
    mine = jnp.where(own, -1.0, 0.0)
    for s in range(count):
        at = (2 * cols_l[s]).astype(F32)
        mine = jnp.where(own & (spot == s), at, mine)
        mine = jnp.where(own & (spot == 32 + s), at + 1.0, mine)
    meta[row] = mine

    y_in.wait()
    pl.semaphore_wait(barrier, n_dev - 1)

    def y_copy(at, to, sem):
        return pltpu.make_async_remote_copy(
            src_ref=ybuf.at[col],
            dst_ref=ybuf.at[at],
            send_sem=ysend.at[sem],
            recv_sem=yrecv.at[at],
            device_id={"col": to},
            device_id_type=MESH,
        )

    each(n_col, lambda k: y_copy(col, lax.rem(col + k, n_col), k).start())

    def row_copy(src, dst, i):
        return pltpu.make_async_remote_copy(
            src_ref=src,
            dst_ref=dst,
            send_sem=rsend.at[i],
            recv_sem=rrecv.at[i],
            device_id={"row": other},
            device_id_type=MESH,
        )

    early = [row_copy(src, prim.at[i, row], i) for i, src in enumerate((x_h, c_h, l_h, u_h))]
    early.append(row_copy(k_h, kind.at[row], 4))
    early.append(row_copy(meta.at[row], meta.at[row], 5))
    for copy in early:
        copy.start()

    scales = [st[si[s]] for s in range(count)]
    scale8, row8, col8 = [], [], []
    for g in range(groups):
        sc = jnp.zeros((8, LANES), F32)
        rr = jnp.zeros((8, LANES), jnp.int32)
        cc = jnp.zeros((8, LANES), jnp.int32)
        for t in range(8):
            s = g * 8 + t
            sc = jnp.where(sub8 == t, scales[s], sc)
            rr = jnp.where(sub8 == t, 2 * rows_l[s], rr)
            cc = jnp.where(sub8 == t, 2 * cols_l[s], cc)
        scale8.append(jnp.concatenate([sc, sc], axis=1))
        row8.append(rr)
        col8.append(cc)

    wide_rows = ybuf.shape[1] * n_col
    tgt_y = jnp.concatenate(row8 + [jnp.full((8, LANES), -2, jnp.int32)], axis=0)
    reps = max(1, wide_rows // LANES)
    if wide_rows < LANES:
        tgt_y = tgt_y[:, :wide_rows]
    else:
        tgt_y = jnp.concatenate([tgt_y] * reps, axis=1)
    lane_y = iota(tgt_y.shape, 1)
    pick_y = [(lane_y == tgt_y + h).astype(F32).astype(BF16) for h in range(2)]

    tgt_p = jnp.concatenate([v for cc in col8 for v in (cc, cc + 2 * col_span)], axis=0)
    reps = 4 * col_span // LANES
    tgt_p = jnp.concatenate([tgt_p] * reps, axis=1)
    lane_p = iota(tgt_p.shape, 1)
    pick_p = [(lane_p == tgt_p + h).astype(F32).astype(BF16) for h in range(2)]

    spot3 = lane256 % (2 * count)
    live = lane256 < 6 * count
    tgt_r = jnp.full((8, 2 * LANES), -1, jnp.int32)
    for s in range(count):
        tgt_r = jnp.where(live & (spot3 == s), 2 * rows_l[s], tgt_r)
        tgt_r = jnp.where(live & (spot3 == count + s), 2 * rows_l[s] + 1, tgt_r)
    place_r = (iota((wide_rows, 2 * LANES), 0) == tgt_r[0:1]).astype(F32).astype(BF16)

    for copy in tile_in:
        copy.wait()
    each(n_col, lambda k: y_copy(lax.rem(col + k, n_col), col, k).wait_recv())

    y_b = ybuf[...].reshape(wide_rows, LANES).astype(BF16)
    y_pick = jnp.concatenate(
        [jnp.dot(pick, y_b, preferred_element_type=F32) for pick in pick_y], axis=1
    )
    sub_y = iota(y_pick.shape, 0)
    lhs = jnp.concatenate(
        [jnp.where(sub_y == s, y_pick, 0.0).astype(BF16) for s in range(count)], axis=1
    )
    product = jnp.dot(lhs, tiles[...].reshape(count * size, size), preferred_element_type=F32)
    product = product * jnp.concatenate(scale8 + [jnp.zeros((8, 2 * LANES), F32)], axis=0)
    part[row, 0] = product[:, :LANES]
    part[row, 1] = product[:, LANES:]
    part_copy = row_copy(part.at[row], part.at[row], 6)
    part_copy.start()

    for copy in small_in:
        copy.wait()
    late = [row_copy(x_h, prim.at[i, other], i) for i in range(4)]
    late.append(row_copy(k_h, kind.at[other], 4))
    late.append(row_copy(meta.at[row], meta.at[other], 5))
    for copy in late:
        copy.wait_recv()
    targets = (meta[0] + meta[1])[0:1]
    place_c = (iota((2 * col_span, LANES), 0).astype(F32) == targets).astype(F32).astype(BF16)
    place_c = jnp.concatenate([place_c] * 3, axis=1)

    row_copy(part.at[row], part.at[other], 6).wait_recv()
    pieces = jnp.concatenate(three_parts(part[...].reshape(LANES, LANES)), axis=0)
    aty = jnp.dot(place_c, pieces, preferred_element_type=F32)

    full = (2 * cblocks, LANES)
    x, c, low, high = [prim[i].reshape(full) for i in range(4)]
    kinds = kind[...].reshape(full)
    reduced = c - aty
    has_low = (kinds == 1) | (kinds == 3)
    has_up = (kinds == 2) | (kinds == 3)
    moved = x - step[0] * reduced
    moved = jnp.where(has_low, jnp.maximum(moved, low), moved)
    x_next = jnp.where(has_up, jnp.minimum(moved, high), moved)
    xn_s[...] = x_next.reshape(xn_s.shape)
    pair = jnp.concatenate([2.0 * x_next - x, x_next], axis=0).astype(BF16)

    p_pick = jnp.concatenate(
        [jnp.dot(pick, pair, preferred_element_type=F32) for pick in pick_p], axis=1
    )
    sub16 = iota((16, size), 0) % 8
    bars, news = [], []
    for g in range(groups):
        rows16 = p_pick[16 * g : 16 * g + 16]
        acc = jnp.zeros((16, size), F32)
        for t in range(8):
            acc = acc + lax.dot_general(
                jnp.where(sub16 == t, rows16, 0.0).astype(BF16),
                tiles[8 * g + t],
                (((1,), (1,)), ((), ())),
                preferred_element_type=F32,
            )
        bars.append(acc[:8] * scale8[g])
        news.append(acc[8:] * scale8[g])
    bar = jnp.concatenate(bars, axis=0)
    new = jnp.concatenate(news, axis=0)
    stacked = jnp.concatenate(
        [
            jnp.concatenate([bar[:, :LANES], new[:, :LANES]], axis=1),
            jnp.concatenate([bar[:, LANES:], new[:, LANES:]], axis=1),
        ],
        axis=0,
    )
    pad = jnp.zeros((2 * LANES - 6 * count, 2 * LANES), BF16)
    pieces = jnp.concatenate(three_parts(stacked) + (pad,), axis=0)
    terms[...] = jnp.dot(place_r, pieces, preferred_element_type=F32).reshape(terms.shape)

    def t_copy(src, at, to, sem):
        return pltpu.make_async_remote_copy(
            src_ref=terms.at[src],
            dst_ref=rt.at[at],
            send_sem=tsend.at[sem],
            recv_sem=trecv.at[at],
            device_id={"col": to},
            device_id_type=MESH,
        )

    def t_start(k):
        to = lax.rem(col + k, n_col)
        t_copy(to, col, to, k).start()

    each(n_col, t_start)
    rt[col] = terms[col]

    xn_out = pltpu.make_async_copy(xn_s.at[row], xn_o, lsem.at[12])
    xn_out.start()
    resid = jnp.where(
        kinds == 0,
        reduced,
        jnp.where(
            kinds == 1,
            jnp.minimum(reduced, 0.0),
            jnp.where(kinds == 2, jnp.maximum(reduced, 0.0), 0.0),
        ),
    )
    bounds = jnp.where(has_low, low * jnp.maximum(reduced, 0.0), 0.0) + jnp.where(
        has_up, high * jnp.minimum(reduced, 0.0), 0.0
    )
    y = ybuf[col]
    b = bbuf[...]
    dual_sum = 0.5 * jnp.sum(resid * resid, axis=0, keepdims=True)
    gap = 0.5 * jnp.sum(c * x_next - bounds, axis=0, keepdims=True) - jnp.sum(
        b * y, axis=0, keepdims=True
    )
    ineq = ebuf[...] == 1

    def t_wait(k):
        t_copy(0, lax.rem(col + k, n_col), col, k).wait_recv()

    each(n_col, t_wait)
    totals = jnp.sum(rt[...], axis=0)
    y_next = y + step[1] * (b - totals[:, :LANES])
    yn_s[...] = jnp.where(ineq, jnp.maximum(y_next, 0.0), y_next)
    p_resid = b - totals[:, LANES:]
    p_resid = jnp.where(ineq, jnp.maximum(p_resid, 0.0), p_resid)
    primal_sum = jnp.sum(p_resid * p_resid, axis=0, keepdims=True)
    sbuf[dev] = jnp.where(
        sub8 == 0, primal_sum, jnp.where(sub8 == 1, dual_sum, jnp.where(sub8 == 2, gap, 0.0))
    )

    def s_copy(at, to, sem):
        return pltpu.make_async_remote_copy(
            src_ref=sbuf.at[dev],
            dst_ref=sbuf.at[at],
            send_sem=ssend.at[sem],
            recv_sem=srecv.at[at],
            device_id={"col": lax.div(to, n_row), "row": lax.rem(to, n_row)},
            device_id_type=MESH,
        )

    each(n_dev, lambda k: s_copy(dev, lax.rem(dev + k, n_dev), k).start())
    yn_out = pltpu.make_async_copy(yn_s, yn_o, lsem.at[13])
    yn_out.start()
    for copy in early:
        copy.wait_send()
    part_copy.wait_send()
    each(n_col, lambda k: y_copy(col, col, k).wait_send())
    each(n_col, lambda k: t_copy(0, col, col, k).wait_send())
    xn_out.wait()
    yn_out.wait()

    each(n_dev, lambda k: s_copy(lax.rem(dev + k, n_dev), dev, k).wait_recv())
    sums = jnp.sum(jnp.sum(sbuf[...], axis=0), axis=1, keepdims=True)
    rows_total = ybuf.shape[1] * LANES * n_dev
    cols_total = cblocks * LANES * n_dev
    lane1 = iota((1, LANES), 1)
    stat_o[...] = jnp.where(
        lane1 == 0,
        sums[0:1] / rows_total,
        jnp.where(lane1 == 1, sums[1:2] / cols_total, sums[2:3] / math.sqrt(cols_total)),
    )
    each(n_dev, lambda k: s_copy(dev, dev, k).wait_send())


def shards(
    tile_values,
    tile_blocks,
    scale_index,
    scale_table,
    primal_iter,
    dual_iter,
    objective,
    right_side,
    lower_bound,
    upper_bound,
    bound_kind,
    row_kind,
    step_sizes,
):
    n_col = lax.axis_size("col")
    n_row = lax.axis_size("row")
    n_dev = n_col * n_row
    count, size, _ = tile_values.shape
    cb = primal_iter.shape[1] // LANES
    rb = dual_iter.shape[1] // LANES
    wide = lambda a: a.reshape(-1, LANES)
    hbm = pl.BlockSpec(memory_space=pltpu.HBM)
    smem = pl.BlockSpec(memory_space=pltpu.SMEM)
    vmem = pl.BlockSpec(memory_space=pltpu.VMEM)
    dma = pltpu.SemaphoreType.DMA
    x_next, y_next, stats = pl.pallas_call(
        functools.partial(kernel, n_col, n_row),
        out_shape=(
            jax.ShapeDtypeStruct((cb, LANES), F32),
            jax.ShapeDtypeStruct((rb, LANES), F32),
            jax.ShapeDtypeStruct((1, LANES), F32),
        ),
        in_specs=[hbm, smem, smem, smem, hbm, hbm, hbm, hbm, hbm, hbm, hbm, hbm, smem],
        out_specs=(hbm, hbm, vmem),
        scratch_shapes=[
            pltpu.VMEM((count, size, size), BF16),
            pltpu.VMEM((4, n_row, cb, LANES), F32),
            pltpu.VMEM((n_row, cb, LANES), jnp.int32),
            pltpu.VMEM((n_col, rb, LANES), F32),
            pltpu.VMEM((rb, LANES), F32),
            pltpu.VMEM((rb, LANES), jnp.int32),
            pltpu.VMEM((n_row, 8, LANES), F32),
            pltpu.VMEM((n_row, 2, 32, LANES), F32),
            pltpu.VMEM((n_row, cb, LANES), F32),
            pltpu.VMEM((rb, LANES), F32),
            pltpu.VMEM((n_col, rb, 2 * LANES), F32),
            pltpu.VMEM((n_col, rb, 2 * LANES), F32),
            pltpu.VMEM((n_dev, 8, LANES), F32),
            dma((14,)),
            dma((n_col,)),
            dma((n_col,)),
            dma((7,)),
            dma((7,)),
            dma((n_col,)),
            dma((n_col,)),
            dma((n_dev,)),
            dma((n_dev,)),
        ],
        compiler_params=pltpu.CompilerParams(
            collective_id=0, has_side_effects=True, vmem_limit_bytes=64 * 1024 * 1024
        ),
    )(
        tile_values,
        tile_blocks.T,
        scale_index,
        scale_table,
        wide(primal_iter),
        wide(dual_iter),
        wide(objective),
        wide(right_side),
        wide(lower_bound),
        wide(upper_bound),
        wide(bound_kind),
        wide(row_kind),
        step_sizes,
    )
    return (x_next.reshape(1, -1), y_next.reshape(1, -1), stats[0, :3])


def solution(mesh):
    return jax.shard_map(
        shards,
        mesh=mesh,
        in_specs=(
            P(("group", "col", "row"), None, None),
            P(("group", "col", "row"), None),
            P(("group", "col", "row")),
            P("group"),
            P(("group", "col"), "row"),
            P(("group", "row"), "col"),
            P(("group", "col"), "row"),
            P(("group", "row"), "col"),
            P(("group", "col"), "row"),
            P(("group", "col"), "row"),
            P(("group", "col"), "row"),
            P(("group", "row"), "col"),
            P("group"),
        ),
        out_specs=(P(("group", "col"), "row"), P(("group", "row"), "col"), P("group")),
        check_vma=False,
    )
```

```python
import functools
import math

import jax
import jax.numpy as jnp
from jax import lax
from jax.experimental import pallas as pl
from jax.experimental.pallas import tpu as pltpu
from jax.sharding import PartitionSpec as P

F32 = jnp.float32
BF16 = jnp.bfloat16
MESH = pl.DeviceIdType.MESH
LANES = 128


def each(count, body):
    if count <= 17:
        for k in range(1, count):
            body(k)
    else:
        lax.fori_loop(1, count, lambda k, _: (body(k), 0)[1], 0)


def three_parts(v):
    hi = v.astype(BF16)
    rest = v - hi.astype(F32)
    mid = rest.astype(BF16)
    low = (rest - mid.astype(F32)).astype(BF16)
    return hi, mid, low


def total(v):
    return jnp.sum(jnp.sum(v, axis=0, keepdims=True), axis=1, keepdims=True)


def iota(shape, dim):
    return lax.broadcasted_iota(jnp.int32, shape, dim)


def kernel(
    n_col,
    n_row,
    tv, tb_h, si_h, st_h, x_h, y_h, c_h, b_h, l_h, u_h, k_h, e_h, step_h,
    xn_o, yn_o, stat_o,
    tiles, prim, kind, ybuf, bbuf, ebuf, meta, part, xn_s, yn_s, terms, rt, sbuf,
    tb, si, st, step, lsem, ysend, yrecv, rsend, rrecv, tsend, trecv, ssend, srecv,
):
    count, size, _ = tv.shape
    groups = count // 8
    cblocks = prim.shape[2]
    n_dev = n_col * n_row
    col = lax.axis_index("col")
    row = lax.axis_index("row")
    other = 1 - row
    dev = col * n_row + row
    row_span = ybuf.shape[1] // 2 * n_col
    col_span = cblocks

    barrier = pltpu.get_barrier_semaphore()

    def greet(k):
        q = lax.rem(dev + k, n_dev)
        pl.semaphore_signal(
            barrier,
            inc=1,
            device_id={"col": lax.div(q, n_row), "row": lax.rem(q, n_row)},
            device_id_type=MESH,
        )

    each(n_dev, greet)

    y_in = pltpu.make_async_copy(y_h, ybuf.at[col], lsem.at[0])
    y_in.start()
    scalar_in = [
        pltpu.make_async_copy(src, dst, lsem.at[14 + i])
        for i, (src, dst) in enumerate(((tb_h, tb), (si_h, si), (st_h, st), (step_h, step)))
    ]
    for copy in scalar_in:
        copy.start()
    chunk = count // 4
    tile_in = []
    for i in range(4):
        span = pl.ds(i * chunk, chunk)
        copy = pltpu.make_async_copy(tv.at[span], tiles.at[span], lsem.at[1 + i])
        copy.start()
        tile_in.append(copy)
    small_in = [
        pltpu.make_async_copy(src, prim.at[i, row], lsem.at[5 + i])
        for i, src in enumerate((x_h, c_h, l_h, u_h))
    ]
    small_in.append(pltpu.make_async_copy(k_h, kind.at[row], lsem.at[9]))
    small_in.append(pltpu.make_async_copy(b_h, bbuf, lsem.at[10]))
    small_in.append(pltpu.make_async_copy(e_h, ebuf, lsem.at[11]))
    for copy in small_in:
        copy.start()

    for copy in scalar_in:
        copy.wait()
    sub8 = iota((8, LANES), 0)
    lane8 = iota((8, LANES), 1)
    lane256 = iota((8, 2 * LANES), 1)
    rows_l = [tb[0, s] - row * row_span for s in range(count)]
    cols_l = [tb[1, s] - col * col_span for s in range(count)]
    own = lane8 // 64 == row
    spot = lane8 % 64
    mine = jnp.where(own, -1.0, 0.0)
    for s in range(count):
        at = (2 * cols_l[s]).astype(F32)
        mine = jnp.where(own & (spot == s), at, mine)
        mine = jnp.where(own & (spot == 32 + s), at + 1.0, mine)
    meta[row] = mine

    y_in.wait()
    pl.semaphore_wait(barrier, n_dev - 1)

    def y_copy(at, to, sem):
        return pltpu.make_async_remote_copy(
            src_ref=ybuf.at[col],
            dst_ref=ybuf.at[at],
            send_sem=ysend.at[sem],
            recv_sem=yrecv.at[at],
            device_id={"col": to},
            device_id_type=MESH,
        )

    each(n_col, lambda k: y_copy(col, lax.rem(col + k, n_col), k).start())

    def row_copy(src, dst, i):
        return pltpu.make_async_remote_copy(
            src_ref=src,
            dst_ref=dst,
            send_sem=rsend.at[i],
            recv_sem=rrecv.at[i],
            device_id={"row": other},
            device_id_type=MESH,
        )

    early = [row_copy(src, prim.at[i, row], i) for i, src in enumerate((x_h, c_h, l_h, u_h))]
    early.append(row_copy(k_h, kind.at[row], 4))
    early.append(row_copy(meta.at[row], meta.at[row], 5))
    for copy in early:
        copy.start()

    scales = [st[si[s]] for s in range(count)]
    scale8, row8, col8 = [], [], []
    for g in range(groups):
        sc = jnp.zeros((8, LANES), F32)
        rr = jnp.zeros((8, LANES), jnp.int32)
        cc = jnp.zeros((8, LANES), jnp.int32)
        for t in range(8):
            s = g * 8 + t
            sc = jnp.where(sub8 == t, scales[s], sc)
            rr = jnp.where(sub8 == t, 2 * rows_l[s], rr)
            cc = jnp.where(sub8 == t, 2 * cols_l[s], cc)
        scale8.append(jnp.concatenate([sc, sc], axis=1))
        row8.append(rr)
        col8.append(cc)

    wide_rows = ybuf.shape[1] * n_col
    tgt_y = jnp.concatenate(row8 + [jnp.full((8, LANES), -2, jnp.int32)], axis=0)
    reps = max(1, wide_rows // LANES)
    if wide_rows < LANES:
        tgt_y = tgt_y[:, :wide_rows]
    else:
        tgt_y = jnp.concatenate([tgt_y] * reps, axis=1)
    lane_y = iota(tgt_y.shape, 1)
    pick_y = [(lane_y == tgt_y + h).astype(F32).astype(BF16) for h in range(2)]

    tgt_p = jnp.concatenate([v for cc in col8 for v in (cc, cc + 2 * col_span)], axis=0)
    reps = 4 * col_span // LANES
    tgt_p = jnp.concatenate([tgt_p] * reps, axis=1)
    lane_p = iota(tgt_p.shape, 1)
    pick_p = [(lane_p == tgt_p + h).astype(F32).astype(BF16) for h in range(2)]

    spot3 = lane256 % (2 * count)
    live = lane256 < 6 * count
    tgt_r = jnp.full((8, 2 * LANES), -1, jnp.int32)
    for s in range(count):
        tgt_r = jnp.where(live & (spot3 == s), 2 * rows_l[s], tgt_r)
        tgt_r = jnp.where(live & (spot3 == count + s), 2 * rows_l[s] + 1, tgt_r)
    place_r = (iota((wide_rows, 2 * LANES), 0) == tgt_r[0:1]).astype(F32).astype(BF16)

    for copy in tile_in:
        copy.wait()
    each(n_col, lambda k: y_copy(lax.rem(col + k, n_col), col, k).wait_recv())

    y_b = ybuf[...].reshape(wide_rows, LANES).astype(BF16)
    y_pick = jnp.concatenate(
        [jnp.dot(pick, y_b, preferred_element_type=F32) for pick in pick_y], axis=1
    )
    sub_y = iota(y_pick.shape, 0)
    lhs = jnp.concatenate(
        [jnp.where(sub_y == s, y_pick, 0.0).astype(BF16) for s in range(count)], axis=1
    )
    product = jnp.dot(lhs, tiles[...].reshape(count * size, size), preferred_element_type=F32)
    product = product * jnp.concatenate(scale8 + [jnp.zeros((8, 2 * LANES), F32)], axis=0)
    part[row, 0] = product[:, :LANES]
    part[row, 1] = product[:, LANES:]
    part_copy = row_copy(part.at[row], part.at[row], 6)
    part_copy.start()

    for copy in small_in:
        copy.wait()
    late = [row_copy(x_h, prim.at[i, other], i) for i in range(4)]
    late.append(row_copy(k_h, kind.at[other], 4))
    late.append(row_copy(meta.at[row], meta.at[other], 5))
    for copy in late:
        copy.wait_recv()
    targets = (meta[0] + meta[1])[0:1]
    place_c = (iota((2 * col_span, LANES), 0).astype(F32) == targets).astype(F32).astype(BF16)
    place_c = jnp.concatenate([place_c] * 3, axis=1)

    row_copy(part.at[row], part.at[other], 6).wait_recv()
    pieces = jnp.concatenate(three_parts(part[...].reshape(LANES, LANES)), axis=0)
    aty = jnp.dot(place_c, pieces, preferred_element_type=F32)

    full = (2 * cblocks, LANES)
    x, c, low, high = [prim[i].reshape(full) for i in range(4)]
    kinds = kind[...].reshape(full)
    reduced = c - aty
    has_low = (kinds == 1) | (kinds == 3)
    has_up = (kinds == 2) | (kinds == 3)
    moved = x - step[0] * reduced
    moved = jnp.where(has_low, jnp.maximum(moved, low), moved)
    x_next = jnp.where(has_up, jnp.minimum(moved, high), moved)
    xn_s[...] = x_next.reshape(xn_s.shape)
    pair = jnp.concatenate([2.0 * x_next - x, x_next], axis=0).astype(BF16)

    p_pick = jnp.concatenate(
        [jnp.dot(pick, pair, preferred_element_type=F32) for pick in pick_p], axis=1
    )
    sub16 = iota((16, size), 0) % 8
    bars, news = [], []
    for g in range(groups):
        rows16 = p_pick[16 * g : 16 * g + 16]
        acc = jnp.zeros((16, size), F32)
        for t in range(8):
            acc = acc + lax.dot_general(
                jnp.where(sub16 == t, rows16, 0.0).astype(BF16),
                tiles[8 * g + t],
                (((1,), (1,)), ((), ())),
                preferred_element_type=F32,
            )
        bars.append(acc[:8] * scale8[g])
        news.append(acc[8:] * scale8[g])
    bar = jnp.concatenate(bars, axis=0)
    new = jnp.concatenate(news, axis=0)
    stacked = jnp.concatenate(
        [
            jnp.concatenate([bar[:, :LANES], new[:, :LANES]], axis=1),
            jnp.concatenate([bar[:, LANES:], new[:, LANES:]], axis=1),
        ],
        axis=0,
    )
    pad = jnp.zeros((2 * LANES - 6 * count, 2 * LANES), BF16)
    pieces = jnp.concatenate(three_parts(stacked) + (pad,), axis=0)
    terms[...] = jnp.dot(place_r, pieces, preferred_element_type=F32).reshape(terms.shape)

    def t_copy(src, at, to, sem):
        return pltpu.make_async_remote_copy(
            src_ref=terms.at[src],
            dst_ref=rt.at[at],
            send_sem=tsend.at[sem],
            recv_sem=trecv.at[at],
            device_id={"col": to},
            device_id_type=MESH,
        )

    def t_start(k):
        to = lax.rem(col + k, n_col)
        t_copy(to, col, to, k).start()

    each(n_col, t_start)
    rt[col] = terms[col]

    xn_out = pltpu.make_async_copy(xn_s.at[row], xn_o, lsem.at[12])
    xn_out.start()
    resid = jnp.where(
        kinds == 0,
        reduced,
        jnp.where(
            kinds == 1,
            jnp.minimum(reduced, 0.0),
            jnp.where(kinds == 2, jnp.maximum(reduced, 0.0), 0.0),
        ),
    )
    bounds = jnp.where(has_low, low * jnp.maximum(reduced, 0.0), 0.0) + jnp.where(
        has_up, high * jnp.minimum(reduced, 0.0), 0.0
    )
    y = ybuf[col]
    b = bbuf[...]
    dual_sum = 0.5 * total(resid * resid)
    gap = 0.5 * total(c * x_next - bounds) - total(b * y)
    lane1 = iota((1, LANES), 1)
    rows_total = ybuf.shape[1] * LANES * n_dev
    cols_total = cblocks * LANES * n_dev
    early_stats = jnp.where(
        lane1 == 1, dual_sum / cols_total, jnp.where(lane1 == 2, gap / math.sqrt(cols_total), 0.0)
    )
    ineq = ebuf[...] == 1

    def t_wait(k):
        t_copy(0, lax.rem(col + k, n_col), col, k).wait_recv()

    each(n_col, t_wait)
    totals = jnp.sum(rt[...], axis=0)
    y_next = y + step[1] * (b - totals[:, :LANES])
    yn_s[...] = jnp.where(ineq, jnp.maximum(y_next, 0.0), y_next)
    p_resid = b - totals[:, LANES:]
    p_resid = jnp.where(ineq, jnp.maximum(p_resid, 0.0), p_resid)
    sbuf[dev] = jnp.where(lane1 == 0, total(p_resid * p_resid) / rows_total, early_stats)

    def s_copy(at, to, sem):
        return pltpu.make_async_remote_copy(
            src_ref=sbuf.at[dev],
            dst_ref=sbuf.at[at],
            send_sem=ssend.at[sem],
            recv_sem=srecv.at[at],
            device_id={"col": lax.div(to, n_row), "row": lax.rem(to, n_row)},
            device_id_type=MESH,
        )

    each(n_dev, lambda k: s_copy(dev, lax.rem(dev + k, n_dev), k).start())
    yn_out = pltpu.make_async_copy(yn_s, yn_o, lsem.at[13])
    yn_out.start()
    for copy in early:
        copy.wait_send()
    part_copy.wait_send()
    each(n_col, lambda k: y_copy(col, col, k).wait_send())
    each(n_col, lambda k: t_copy(0, col, col, k).wait_send())
    xn_out.wait()
    yn_out.wait()

    each(n_dev, lambda k: s_copy(lax.rem(dev + k, n_dev), dev, k).wait_recv())
    stat_o[...] = jnp.sum(sbuf[...], axis=0)
    each(n_dev, lambda k: s_copy(dev, dev, k).wait_send())


def hand_on(x_i, y_i, stat_i, x_o, y_o, stat_o):
    x_o[...] = x_i[...]
    y_o[...] = y_i[...]
    stat_o[...] = stat_i[0, :3]


def shards(
    tile_values,
    tile_blocks,
    scale_index,
    scale_table,
    primal_iter,
    dual_iter,
    objective,
    right_side,
    lower_bound,
    upper_bound,
    bound_kind,
    row_kind,
    step_sizes,
):
    n_col = lax.axis_size("col")
    n_row = lax.axis_size("row")
    n_dev = n_col * n_row
    count, size, _ = tile_values.shape
    cb = primal_iter.shape[1] // LANES
    rb = dual_iter.shape[1] // LANES
    wide = lambda a: a.reshape(-1, LANES)
    hbm = pl.BlockSpec(memory_space=pltpu.HBM)
    vmem = pl.BlockSpec(memory_space=pltpu.VMEM)
    dma = pltpu.SemaphoreType.DMA
    x_next, y_next, stats = pl.pallas_call(
        functools.partial(kernel, n_col, n_row),
        out_shape=(
            jax.ShapeDtypeStruct((cb, LANES), F32),
            jax.ShapeDtypeStruct((rb, LANES), F32),
            jax.ShapeDtypeStruct((1, LANES), F32),
        ),
        in_specs=[hbm] * 13,
        out_specs=(hbm, hbm, vmem),
        scratch_shapes=[
            pltpu.VMEM((count, size, size), BF16),
            pltpu.VMEM((4, n_row, cb, LANES), F32),
            pltpu.VMEM((n_row, cb, LANES), jnp.int32),
            pltpu.VMEM((n_col, rb, LANES), F32),
            pltpu.VMEM((rb, LANES), F32),
            pltpu.VMEM((rb, LANES), jnp.int32),
            pltpu.VMEM((n_row, 8, LANES), F32),
            pltpu.VMEM((n_row, 2, 32, LANES), F32),
            pltpu.VMEM((n_row, cb, LANES), F32),
            pltpu.VMEM((rb, LANES), F32),
            pltpu.VMEM((n_col, rb, 2 * LANES), F32),
            pltpu.VMEM((n_col, rb, 2 * LANES), F32),
            pltpu.VMEM((n_dev, 1, LANES), F32),
            pltpu.SMEM((2, count), jnp.int32),
            pltpu.SMEM(scale_index.shape, jnp.int32),
            pltpu.SMEM(scale_table.shape, F32),
            pltpu.SMEM(step_sizes.shape, F32),
            dma((18,)),
            dma((n_col,)),
            dma((n_col,)),
            dma((7,)),
            dma((7,)),
            dma((n_col,)),
            dma((n_col,)),
            dma((n_dev,)),
            dma((n_dev,)),
        ],
        compiler_params=pltpu.CompilerParams(
            collective_id=0, has_side_effects=True, vmem_limit_bytes=64 * 1024 * 1024
        ),
    )(
        tile_values,
        tile_blocks.T,
        scale_index,
        scale_table,
        wide(primal_iter),
        wide(dual_iter),
        wide(objective),
        wide(right_side),
        wide(lower_bound),
        wide(upper_bound),
        wide(bound_kind),
        wide(row_kind),
        step_sizes,
    )
    x_next, y_next, stats = pl.pallas_call(
        hand_on,
        out_shape=(
            jax.ShapeDtypeStruct((cb, LANES), F32),
            jax.ShapeDtypeStruct((rb, LANES), F32),
            jax.ShapeDtypeStruct((3,), F32),
        ),
        in_specs=[vmem] * 3,
        out_specs=(vmem, vmem, vmem),
        scratch_shapes=[],
        compiler_params=pltpu.CompilerParams(vmem_limit_bytes=64 * 1024 * 1024),
    )(x_next, y_next, stats)
    return (x_next.reshape(1, -1), y_next.reshape(1, -1), stats)


def solution(mesh):
    return jax.shard_map(
        shards,
        mesh=mesh,
        in_specs=(
            P(("group", "col", "row"), None, None),
            P(("group", "col", "row"), None),
            P(("group", "col", "row")),
            P("group"),
            P(("group", "col"), "row"),
            P(("group", "row"), "col"),
            P(("group", "col"), "row"),
            P(("group", "row"), "col"),
            P(("group", "col"), "row"),
            P(("group", "col"), "row"),
            P(("group", "col"), "row"),
            P(("group", "row"), "col"),
            P("group"),
        ),
        out_specs=(P(("group", "col"), "row"), P(("group", "row"), "col"), P("group")),
        check_vma=False,
    )
```

```python
import functools
import math

import jax
import jax.numpy as jnp
from jax import lax
from jax.experimental import pallas as pl
from jax.experimental.pallas import tpu as pltpu
from jax.sharding import PartitionSpec as P

F32 = jnp.float32
BF16 = jnp.bfloat16
MESH = pl.DeviceIdType.MESH
LANES = 128


def each(count, body):
    if count <= 17:
        for k in range(1, count):
            body(k)
    else:
        lax.fori_loop(1, count, lambda k, _: (body(k), 0)[1], 0)


def three_parts(v):
    hi = v.astype(BF16)
    rest = v - hi.astype(F32)
    mid = rest.astype(BF16)
    low = (rest - mid.astype(F32)).astype(BF16)
    return hi, mid, low


def far_first(me, count, k):
    j = k - 1
    up = lax.div(2 * me, count)
    rising = j + lax.div(j + count - me, count)
    falling = count - 1 - j - lax.div(j + 1 + me, count)
    return up * rising + (1 - up) * falling


def total(v):
    return jnp.sum(jnp.sum(v, axis=0, keepdims=True), axis=1, keepdims=True)


def iota(shape, dim):
    return lax.broadcasted_iota(jnp.int32, shape, dim)


def kernel(
    n_col,
    n_row,
    tv, tb_h, si_h, st_h, x_h, y_h, c_h, b_h, l_h, u_h, k_h, e_h, step_h,
    xn_o, yn_o, stat_o,
    tiles, flipped, prim, kind, ybuf, bbuf, ebuf, meta, part, xn_s, yn_s, terms, rt, sbuf,
    tb, si, st, step, lsem, ysend, yrecv, rsend, rrecv, tsend, trecv, ssend, srecv,
):
    count, size, _ = tv.shape
    groups = count // 8
    cblocks = prim.shape[2]
    n_dev = n_col * n_row
    col = lax.axis_index("col")
    row = lax.axis_index("row")
    other = 1 - row
    dev = col * n_row + row
    row_span = ybuf.shape[1] // 2 * n_col
    col_span = cblocks

    barrier = pltpu.get_barrier_semaphore()

    def greet(k):
        q = far_first(dev, n_dev, k)
        pl.semaphore_signal(
            barrier,
            inc=1,
            device_id={"col": lax.div(q, n_row), "row": lax.rem(q, n_row)},
            device_id_type=MESH,
        )

    each(n_dev, greet)

    y_in = pltpu.make_async_copy(y_h, ybuf.at[col], lsem.at[0])
    y_in.start()
    scalar_in = [
        pltpu.make_async_copy(src, dst, lsem.at[14 + i])
        for i, (src, dst) in enumerate(((tb_h, tb), (si_h, si), (st_h, st), (step_h, step)))
    ]
    for copy in scalar_in:
        copy.start()
    chunk = count // 4
    tile_in = []
    for i in range(4):
        span = pl.ds(i * chunk, chunk)
        copy = pltpu.make_async_copy(tv.at[span], tiles.at[span], lsem.at[1 + i])
        copy.start()
        tile_in.append(copy)
    small_in = [
        pltpu.make_async_copy(src, prim.at[i, row], lsem.at[5 + i])
        for i, src in enumerate((x_h, c_h, l_h, u_h))
    ]
    small_in.append(pltpu.make_async_copy(k_h, kind.at[row], lsem.at[9]))
    small_in.append(pltpu.make_async_copy(b_h, bbuf, lsem.at[10]))
    small_in.append(pltpu.make_async_copy(e_h, ebuf, lsem.at[11]))
    for copy in small_in:
        copy.start()

    for copy in scalar_in:
        copy.wait()
    sub8 = iota((8, LANES), 0)
    lane8 = iota((8, LANES), 1)
    lane256 = iota((8, 2 * LANES), 1)
    rows_l = [tb[0, s] - row * row_span for s in range(count)]
    cols_l = [tb[1, s] - col * col_span for s in range(count)]
    own = lane8 // 64 == row
    spot = lane8 % 64
    mine = jnp.where(own, -1.0, 0.0)
    for s in range(count):
        at = (2 * cols_l[s]).astype(F32)
        mine = jnp.where(own & (spot == s), at, mine)
        mine = jnp.where(own & (spot == 32 + s), at + 1.0, mine)
    meta[row] = mine

    y_in.wait()
    pl.semaphore_wait(barrier, n_dev - 1)

    def y_copy(at, to, sem):
        return pltpu.make_async_remote_copy(
            src_ref=ybuf.at[col],
            dst_ref=ybuf.at[at],
            send_sem=ysend.at[sem],
            recv_sem=yrecv.at[at],
            device_id={"col": to},
            device_id_type=MESH,
        )

    each(n_col, lambda k: y_copy(col, far_first(col, n_col, k), k).start())

    def row_copy(src, dst, i):
        return pltpu.make_async_remote_copy(
            src_ref=src,
            dst_ref=dst,
            send_sem=rsend.at[i],
            recv_sem=rrecv.at[i],
            device_id={"row": other},
            device_id_type=MESH,
        )

    early = [row_copy(src, prim.at[i, row], i) for i, src in enumerate((x_h, c_h, l_h, u_h))]
    early.append(row_copy(k_h, kind.at[row], 4))
    early.append(row_copy(meta.at[row], meta.at[row], 5))
    for copy in early:
        copy.start()

    scales = [st[si[s]] for s in range(count)]
    scale8, row8, col8 = [], [], []
    for g in range(groups):
        sc = jnp.zeros((8, LANES), F32)
        rr = jnp.zeros((8, LANES), jnp.int32)
        cc = jnp.zeros((8, LANES), jnp.int32)
        for t in range(8):
            s = g * 8 + t
            sc = jnp.where(sub8 == t, scales[s], sc)
            rr = jnp.where(sub8 == t, 2 * rows_l[s], rr)
            cc = jnp.where(sub8 == t, 2 * cols_l[s], cc)
        scale8.append(jnp.concatenate([sc, sc], axis=1))
        row8.append(rr)
        col8.append(cc)

    wide_rows = ybuf.shape[1] * n_col
    tgt_y = jnp.concatenate(row8 + [jnp.full((8, LANES), -2, jnp.int32)], axis=0)
    reps = max(1, wide_rows // LANES)
    if wide_rows < LANES:
        tgt_y = tgt_y[:, :wide_rows]
    else:
        tgt_y = jnp.concatenate([tgt_y] * reps, axis=1)
    lane_y = iota(tgt_y.shape, 1)
    pick_y = [(lane_y == tgt_y + h).astype(F32).astype(BF16) for h in range(2)]

    tgt_p = jnp.concatenate([v for cc in col8 for v in (cc, cc + 2 * col_span)], axis=0)
    reps = 4 * col_span // LANES
    tgt_p = jnp.concatenate([tgt_p] * reps, axis=1)
    lane_p = iota(tgt_p.shape, 1)
    pick_p = [(lane_p == tgt_p + h).astype(F32).astype(BF16) for h in range(2)]

    spot3 = lane256 % (2 * count)
    live = lane256 < 6 * count
    tgt_r = jnp.full((8, 2 * LANES), -1, jnp.int32)
    for s in range(count):
        tgt_r = jnp.where(live & (spot3 == s), 2 * rows_l[s], tgt_r)
        tgt_r = jnp.where(live & (spot3 == count + s), 2 * rows_l[s] + 1, tgt_r)
    place_r = (iota((wide_rows, 2 * LANES), 0) == tgt_r[0:1]).astype(F32).astype(BF16)

    for copy in tile_in:
        copy.wait()
    for s in range(count):
        flipped[s * size : (s + 1) * size] = tiles[s].T
    each(n_col, lambda k: y_copy(lax.rem(col + k, n_col), col, k).wait_recv())

    y_b = ybuf[...].reshape(wide_rows, LANES).astype(BF16)
    y_pick = jnp.concatenate(
        [jnp.dot(pick, y_b, preferred_element_type=F32) for pick in pick_y], axis=1
    )
    sub_y = iota(y_pick.shape, 0)
    lhs = jnp.concatenate(
        [jnp.where(sub_y == s, y_pick, 0.0).astype(BF16) for s in range(count)], axis=1
    )
    product = jnp.dot(lhs, tiles[...].reshape(count * size, size), preferred_element_type=F32)
    product = product * jnp.concatenate(scale8 + [jnp.zeros((8, 2 * LANES), F32)], axis=0)
    part[row, 0] = product[:, :LANES]
    part[row, 1] = product[:, LANES:]
    part_copy = row_copy(part.at[row], part.at[row], 6)
    part_copy.start()

    for copy in small_in:
        copy.wait()
    late = [row_copy(x_h, prim.at[i, other], i) for i in range(4)]
    late.append(row_copy(k_h, kind.at[other], 4))
    late.append(row_copy(meta.at[row], meta.at[other], 5))
    for copy in late:
        copy.wait_recv()
    targets = (meta[0] + meta[1])[0:1]
    place_c = (iota((2 * col_span, LANES), 0).astype(F32) == targets).astype(F32).astype(BF16)
    place_c = jnp.concatenate([place_c] * 3, axis=1)

    row_copy(part.at[row], part.at[other], 6).wait_recv()
    pieces = jnp.concatenate(three_parts(part[...].reshape(LANES, LANES)), axis=0)
    aty = jnp.dot(place_c, pieces, preferred_element_type=F32)

    full = (2 * cblocks, LANES)
    x, c, low, high = [prim[i].reshape(full) for i in range(4)]
    kinds = kind[...].reshape(full)
    reduced = c - aty
    has_low = (kinds == 1) | (kinds == 3)
    has_up = (kinds == 2) | (kinds == 3)
    moved = x - step[0] * reduced
    moved = jnp.where(has_low, jnp.maximum(moved, low), moved)
    x_next = jnp.where(has_up, jnp.minimum(moved, high), moved)
    xn_s[...] = x_next.reshape(xn_s.shape)
    pair = jnp.concatenate([2.0 * x_next - x, x_next], axis=0).astype(BF16)

    p_pick = jnp.concatenate(
        [jnp.dot(pick, pair, preferred_element_type=F32) for pick in pick_p], axis=1
    )
    sub_p = iota(p_pick.shape, 0)
    lhs = jnp.concatenate(
        [
            jnp.where((sub_p % 8 == s % 8) & (sub_p // 16 == s // 8), p_pick, 0.0).astype(BF16)
            for s in range(count)
        ],
        axis=1,
    )
    acc = jnp.dot(lhs, flipped[...], preferred_element_type=F32)
    bars = [acc[16 * g : 16 * g + 8] * scale8[g] for g in range(groups)]
    news = [acc[16 * g + 8 : 16 * g + 16] * scale8[g] for g in range(groups)]
    bar = jnp.concatenate(bars, axis=0)
    new = jnp.concatenate(news, axis=0)
    stacked = jnp.concatenate(
        [
            jnp.concatenate([bar[:, :LANES], new[:, :LANES]], axis=1),
            jnp.concatenate([bar[:, LANES:], new[:, LANES:]], axis=1),
        ],
        axis=0,
    )
    pad = jnp.zeros((2 * LANES - 6 * count, 2 * LANES), BF16)
    pieces = jnp.concatenate(three_parts(stacked) + (pad,), axis=0)
    terms[...] = jnp.dot(place_r, pieces, preferred_element_type=F32).reshape(terms.shape)

    def t_copy(src, at, to, sem):
        return pltpu.make_async_remote_copy(
            src_ref=terms.at[src],
            dst_ref=rt.at[at],
            send_sem=tsend.at[sem],
            recv_sem=trecv.at[at],
            device_id={"col": to},
            device_id_type=MESH,
        )

    def t_start(k):
        to = far_first(col, n_col, k)
        t_copy(to, col, to, k).start()

    each(n_col, t_start)
    rt[col] = terms[col]

    xn_out = pltpu.make_async_copy(xn_s.at[row], xn_o, lsem.at[12])
    xn_out.start()
    resid = jnp.where(
        kinds == 0,
        reduced,
        jnp.where(
            kinds == 1,
            jnp.minimum(reduced, 0.0),
            jnp.where(kinds == 2, jnp.maximum(reduced, 0.0), 0.0),
        ),
    )
    bounds = jnp.where(has_low, low * jnp.maximum(reduced, 0.0), 0.0) + jnp.where(
        has_up, high * jnp.minimum(reduced, 0.0), 0.0
    )
    y = ybuf[col]
    b = bbuf[...]
    dual_sum = 0.5 * total(resid * resid)
    gap = 0.5 * total(c * x_next - bounds) - total(b * y)
    lane1 = iota((1, LANES), 1)
    rows_total = ybuf.shape[1] * LANES * n_dev
    cols_total = cblocks * LANES * n_dev
    early_stats = jnp.where(
        lane1 == 1, dual_sum / cols_total, jnp.where(lane1 == 2, gap / math.sqrt(cols_total), 0.0)
    )
    ineq = ebuf[...] == 1

    def t_wait(k):
        t_copy(0, lax.rem(col + k, n_col), col, k).wait_recv()

    each(n_col, t_wait)
    totals = jnp.sum(rt[...], axis=0)
    y_next = y + step[1] * (b - totals[:, :LANES])
    yn_s[...] = jnp.where(ineq, jnp.maximum(y_next, 0.0), y_next)
    p_resid = b - totals[:, LANES:]
    p_resid = jnp.where(ineq, jnp.maximum(p_resid, 0.0), p_resid)
    sbuf[0] = jnp.where(lane1 == 0, total(p_resid * p_resid) / rows_total, early_stats)

    def s_copy(at, to, sem):
        return pltpu.make_async_remote_copy(
            src_ref=sbuf.at[0],
            dst_ref=stat_o.at[at],
            send_sem=ssend.at[sem],
            recv_sem=srecv.at[at],
            device_id={"col": lax.div(to, n_row), "row": lax.rem(to, n_row)},
            device_id_type=MESH,
        )

    each(n_dev, lambda k: s_copy(dev, far_first(dev, n_dev, k), k).start())
    own_stat = pltpu.make_async_copy(sbuf.at[0], stat_o.at[dev], lsem.at[18])
    own_stat.start()
    yn_out = pltpu.make_async_copy(yn_s, yn_o, lsem.at[13])
    yn_out.start()
    for copy in early:
        copy.wait_send()
    part_copy.wait_send()
    each(n_col, lambda k: y_copy(col, col, k).wait_send())
    each(n_col, lambda k: t_copy(0, col, col, k).wait_send())
    xn_out.wait()
    yn_out.wait()

    each(n_dev, lambda k: s_copy(lax.rem(dev + k, n_dev), dev, k).wait_recv())
    own_stat.wait()
    each(n_dev, lambda k: s_copy(dev, dev, k).wait_send())


def hand_on(x_i, y_i, stat_i, x_o, y_o, stat_o):
    x_o[...] = x_i[...]
    y_o[...] = y_i[...]
    stat_o[...] = jnp.sum(stat_i[...], axis=0)[0, :3]


def shards(
    tile_values,
    tile_blocks,
    scale_index,
    scale_table,
    primal_iter,
    dual_iter,
    objective,
    right_side,
    lower_bound,
    upper_bound,
    bound_kind,
    row_kind,
    step_sizes,
):
    n_col = lax.axis_size("col")
    n_row = lax.axis_size("row")
    n_dev = n_col * n_row
    count, size, _ = tile_values.shape
    cb = primal_iter.shape[1] // LANES
    rb = dual_iter.shape[1] // LANES
    wide = lambda a: a.reshape(-1, LANES)
    hbm = pl.BlockSpec(memory_space=pltpu.HBM)
    vmem = pl.BlockSpec(memory_space=pltpu.VMEM)
    dma = pltpu.SemaphoreType.DMA
    x_next, y_next, stats = pl.pallas_call(
        functools.partial(kernel, n_col, n_row),
        out_shape=(
            jax.ShapeDtypeStruct((cb, LANES), F32),
            jax.ShapeDtypeStruct((rb, LANES), F32),
            jax.ShapeDtypeStruct((n_dev, 1, LANES), F32),
        ),
        in_specs=[hbm] * 13,
        out_specs=(hbm, hbm, hbm),
        scratch_shapes=[
            pltpu.VMEM((count, size, size), BF16),
            pltpu.VMEM((count * size, size), BF16),
            pltpu.VMEM((4, n_row, cb, LANES), F32),
            pltpu.VMEM((n_row, cb, LANES), jnp.int32),
            pltpu.VMEM((n_col, rb, LANES), F32),
            pltpu.VMEM((rb, LANES), F32),
            pltpu.VMEM((rb, LANES), jnp.int32),
            pltpu.VMEM((n_row, 8, LANES), F32),
            pltpu.VMEM((n_row, 2, 32, LANES), F32),
            pltpu.VMEM((n_row, cb, LANES), F32),
            pltpu.VMEM((rb, LANES), F32),
            pltpu.VMEM((n_col, rb, 2 * LANES), F32),
            pltpu.VMEM((n_col, rb, 2 * LANES), F32),
            pltpu.VMEM((1, 1, LANES), F32),
            pltpu.SMEM((2, count), jnp.int32),
            pltpu.SMEM(scale_index.shape, jnp.int32),
            pltpu.SMEM(scale_table.shape, F32),
            pltpu.SMEM(step_sizes.shape, F32),
            dma((19,)),
            dma((n_col,)),
            dma((n_col,)),
            dma((7,)),
            dma((7,)),
            dma((n_col,)),
            dma((n_col,)),
            dma((n_dev,)),
            dma((n_dev,)),
        ],
        compiler_params=pltpu.CompilerParams(
            collective_id=0, has_side_effects=True, vmem_limit_bytes=64 * 1024 * 1024
        ),
    )(
        tile_values,
        tile_blocks.T,
        scale_index,
        scale_table,
        wide(primal_iter),
        wide(dual_iter),
        wide(objective),
        wide(right_side),
        wide(lower_bound),
        wide(upper_bound),
        wide(bound_kind),
        wide(row_kind),
        step_sizes,
    )
    x_next, y_next, stats = pl.pallas_call(
        hand_on,
        out_shape=(
            jax.ShapeDtypeStruct((cb, LANES), F32),
            jax.ShapeDtypeStruct((rb, LANES), F32),
            jax.ShapeDtypeStruct((3,), F32),
        ),
        in_specs=[vmem] * 3,
        out_specs=(vmem, vmem, vmem),
        scratch_shapes=[],
        compiler_params=pltpu.CompilerParams(vmem_limit_bytes=64 * 1024 * 1024),
    )(x_next, y_next, stats)
    return (x_next.reshape(1, -1), y_next.reshape(1, -1), stats)


def solution(mesh):
    return jax.shard_map(
        shards,
        mesh=mesh,
        in_specs=(
            P(("group", "col", "row"), None, None),
            P(("group", "col", "row"), None),
            P(("group", "col", "row")),
            P("group"),
            P(("group", "col"), "row"),
            P(("group", "row"), "col"),
            P(("group", "col"), "row"),
            P(("group", "row"), "col"),
            P(("group", "col"), "row"),
            P(("group", "col"), "row"),
            P(("group", "col"), "row"),
            P(("group", "row"), "col"),
            P("group"),
        ),
        out_specs=(P(("group", "col"), "row"), P(("group", "row"), "col"), P("group")),
        check_vma=False,
    )
```

```python
import functools
import math

import jax
import jax.numpy as jnp
from jax import lax
from jax.experimental import pallas as pl
from jax.experimental.pallas import tpu as pltpu
from jax.sharding import PartitionSpec as P

F32 = jnp.float32
BF16 = jnp.bfloat16
MESH = pl.DeviceIdType.MESH
LANES = 128


def each(count, body):
    if count <= 17:
        for k in range(1, count):
            body(k)
    else:
        lax.fori_loop(1, count, lambda k, _: (body(k), 0)[1], 0)


def three_parts(v):
    hi = v.astype(BF16)
    rest = v - hi.astype(F32)
    mid = rest.astype(BF16)
    low = (rest - mid.astype(F32)).astype(BF16)
    return hi, mid, low


def far_first(me, count, k):
    j = k - 1
    up = lax.div(2 * me, count)
    rising = j + lax.div(j + count - me, count)
    falling = count - 1 - j - lax.div(j + 1 + me, count)
    return up * rising + (1 - up) * falling


def total(v):
    return jnp.sum(jnp.sum(v, axis=0, keepdims=True), axis=1, keepdims=True)


def iota(shape, dim):
    return lax.broadcasted_iota(jnp.int32, shape, dim)


def kernel(
    n_col,
    n_row,
    tv, tb_h, si_h, st_h, x_h, y_h, c_h, b_h, l_h, u_h, k_h, e_h, step_h,
    xn_o, yn_o, stat_o,
    tiles, flipped, prim, kind, ybuf, bbuf, ebuf, meta, part, xn_s, yn_s, terms, rt, sbuf,
    tb, si, st, step, lsem, ysend, yrecv, rsend, rrecv, tsend, trecv, ssend, srecv,
):
    count, size, _ = tv.shape
    groups = count // 8
    cblocks = prim.shape[2]
    n_dev = n_col * n_row
    col = lax.axis_index("col")
    row = lax.axis_index("row")
    other = 1 - row
    dev = col * n_row + row
    row_span = ybuf.shape[1] // 2 * n_col
    col_span = cblocks

    barrier = pltpu.get_barrier_semaphore()

    def greet(k):
        q = far_first(dev, n_dev, k)
        pl.semaphore_signal(
            barrier,
            inc=1,
            device_id={"col": lax.div(q, n_row), "row": lax.rem(q, n_row)},
            device_id_type=MESH,
        )

    each(n_dev, greet)

    y_in = pltpu.make_async_copy(y_h, ybuf.at[col], lsem.at[0])
    y_in.start()
    scalar_in = [
        pltpu.make_async_copy(src, dst, lsem.at[14 + i])
        for i, (src, dst) in enumerate(((tb_h, tb), (si_h, si), (st_h, st), (step_h, step)))
    ]
    for copy in scalar_in:
        copy.start()
    chunk = count // 4
    tile_in = []
    for i in range(4):
        span = pl.ds(i * chunk, chunk)
        copy = pltpu.make_async_copy(tv.at[span], tiles.at[span], lsem.at[1 + i])
        copy.start()
        tile_in.append(copy)
    small_in = [
        pltpu.make_async_copy(src, prim.at[i, row], lsem.at[5 + i])
        for i, src in enumerate((x_h, c_h, l_h, u_h))
    ]
    small_in.append(pltpu.make_async_copy(k_h, kind.at[row], lsem.at[9]))
    small_in.append(pltpu.make_async_copy(b_h, bbuf, lsem.at[10]))
    small_in.append(pltpu.make_async_copy(e_h, ebuf, lsem.at[11]))
    for copy in small_in:
        copy.start()

    for copy in scalar_in:
        copy.wait()
    sub8 = iota((8, LANES), 0)
    lane8 = iota((8, LANES), 1)
    lane256 = iota((8, 2 * LANES), 1)
    rows_l = [tb[0, s] - row * row_span for s in range(count)]
    cols_l = [tb[1, s] - col * col_span for s in range(count)]
    own = lane8 // 64 == row
    spot = lane8 % 64
    mine = jnp.where(own, -1.0, 0.0)
    for s in range(count):
        at = (2 * cols_l[s]).astype(F32)
        mine = jnp.where(own & (spot == s), at, mine)
        mine = jnp.where(own & (spot == 32 + s), at + 1.0, mine)
    meta[row] = mine

    y_in.wait()
    pl.semaphore_wait(barrier, n_dev - 1)

    def y_copy(at, to, sem):
        return pltpu.make_async_remote_copy(
            src_ref=ybuf.at[col],
            dst_ref=ybuf.at[at],
            send_sem=ysend.at[sem],
            recv_sem=yrecv.at[at],
            device_id={"col": to},
            device_id_type=MESH,
        )

    each(n_col, lambda k: y_copy(col, far_first(col, n_col, k), k).start())

    def row_copy(src, dst, i):
        return pltpu.make_async_remote_copy(
            src_ref=src,
            dst_ref=dst,
            send_sem=rsend.at[i],
            recv_sem=rrecv.at[i],
            device_id={"row": other},
            device_id_type=MESH,
        )

    early = [row_copy(src, prim.at[i, row], i) for i, src in enumerate((x_h, c_h, l_h, u_h))]
    early.append(row_copy(k_h, kind.at[row], 4))
    early.append(row_copy(meta.at[row], meta.at[row], 5))
    for copy in early:
        copy.start()

    scales = [st[si[s]] for s in range(count)]
    scale8, row8, col8 = [], [], []
    for g in range(groups):
        sc = jnp.zeros((8, LANES), F32)
        rr = jnp.zeros((8, LANES), jnp.int32)
        cc = jnp.zeros((8, LANES), jnp.int32)
        for t in range(8):
            s = g * 8 + t
            sc = jnp.where(sub8 == t, scales[s], sc)
            rr = jnp.where(sub8 == t, 2 * rows_l[s], rr)
            cc = jnp.where(sub8 == t, 2 * cols_l[s], cc)
        scale8.append(jnp.concatenate([sc, sc], axis=1))
        row8.append(rr)
        col8.append(cc)

    wide_rows = ybuf.shape[1] * n_col
    tgt_y = jnp.concatenate(row8 + [jnp.full((8, LANES), -2, jnp.int32)], axis=0)
    reps = max(1, wide_rows // LANES)
    if wide_rows < LANES:
        tgt_y = tgt_y[:, :wide_rows]
    else:
        tgt_y = jnp.concatenate([tgt_y] * reps, axis=1)
    lane_y = iota(tgt_y.shape, 1)
    pick_y = [(lane_y == tgt_y + h).astype(F32).astype(BF16) for h in range(2)]

    tgt_p = jnp.concatenate([v for cc in col8 for v in (cc, cc + 2 * col_span)], axis=0)
    reps = 4 * col_span // LANES
    tgt_p = jnp.concatenate([tgt_p] * reps, axis=1)
    lane_p = iota(tgt_p.shape, 1)
    pick_p = [(lane_p == tgt_p + h).astype(F32).astype(BF16) for h in range(2)]

    spot3 = lane256 % (2 * count)
    live = lane256 < 6 * count
    tgt_r = jnp.full((8, 2 * LANES), -1, jnp.int32)
    for s in range(count):
        tgt_r = jnp.where(live & (spot3 == s), 2 * rows_l[s], tgt_r)
        tgt_r = jnp.where(live & (spot3 == count + s), 2 * rows_l[s] + 1, tgt_r)
    place_r = (iota((wide_rows, 2 * LANES), 0) == tgt_r[0:1]).astype(F32).astype(BF16)

    for copy in tile_in:
        copy.wait()
    for s in range(count):
        flipped[s * size : (s + 1) * size] = tiles[s].T
    each(n_col, lambda k: y_copy(lax.rem(col + k, n_col), col, k).wait_recv())

    y_b = ybuf[...].reshape(wide_rows, LANES).astype(BF16)
    y_pick = jnp.concatenate(
        [jnp.dot(pick, y_b, preferred_element_type=F32) for pick in pick_y], axis=1
    )
    sub_y = iota((8, size), 0)
    product = []
    for g in range(groups):
        rows8 = y_pick[8 * g : 8 * g + 8]
        lhs = jnp.concatenate(
            [jnp.where(sub_y == t, rows8, 0.0) for t in range(8)], axis=1
        ).astype(BF16)
        weights = tiles[8 * g : 8 * g + 8].reshape(8 * size, size)
        product.append(jnp.dot(lhs, weights, preferred_element_type=F32) * scale8[g])
    product = jnp.concatenate(product + [jnp.zeros((8, size), F32)], axis=0)
    part[row, 0] = product[:, :LANES]
    part[row, 1] = product[:, LANES:]
    part_copy = row_copy(part.at[row], part.at[row], 6)
    part_copy.start()

    for copy in small_in:
        copy.wait()
    late = [row_copy(x_h, prim.at[i, other], i) for i in range(4)]
    late.append(row_copy(k_h, kind.at[other], 4))
    late.append(row_copy(meta.at[row], meta.at[other], 5))
    for copy in late:
        copy.wait_recv()
    targets = (meta[0] + meta[1])[0:1]
    place_c = (iota((2 * col_span, LANES), 0).astype(F32) == targets).astype(F32).astype(BF16)
    place_c = jnp.concatenate([place_c] * 3, axis=1)

    row_copy(part.at[row], part.at[other], 6).wait_recv()
    pieces = jnp.concatenate(three_parts(part[...].reshape(LANES, LANES)), axis=0)
    aty = jnp.dot(place_c, pieces, preferred_element_type=F32)

    full = (2 * cblocks, LANES)
    x, c, low, high = [prim[i].reshape(full) for i in range(4)]
    kinds = kind[...].reshape(full)
    reduced = c - aty
    has_low = (kinds == 1) | (kinds == 3)
    has_up = (kinds == 2) | (kinds == 3)
    moved = x - step[0] * reduced
    moved = jnp.where(has_low, jnp.maximum(moved, low), moved)
    x_next = jnp.where(has_up, jnp.minimum(moved, high), moved)
    xn_s[...] = x_next.reshape(xn_s.shape)
    pair = jnp.concatenate([2.0 * x_next - x, x_next], axis=0).astype(BF16)

    p_pick = jnp.concatenate(
        [jnp.dot(pick, pair, preferred_element_type=F32) for pick in pick_p], axis=1
    )
    sub_p = iota((16, size), 0) % 8
    bars, news = [], []
    for g in range(groups):
        rows16 = p_pick[16 * g : 16 * g + 16]
        lhs = jnp.concatenate(
            [jnp.where(sub_p == t, rows16, 0.0).astype(BF16) for t in range(8)], axis=1
        )
        weights = flipped[8 * g * size : 8 * (g + 1) * size]
        acc = jnp.dot(lhs, weights, preferred_element_type=F32)
        bars.append(acc[:8] * scale8[g])
        news.append(acc[8:] * scale8[g])
    bar = jnp.concatenate(bars, axis=0)
    new = jnp.concatenate(news, axis=0)
    stacked = jnp.concatenate(
        [
            jnp.concatenate([bar[:, :LANES], new[:, :LANES]], axis=1),
            jnp.concatenate([bar[:, LANES:], new[:, LANES:]], axis=1),
        ],
        axis=0,
    )
    pad = jnp.zeros((2 * LANES - 6 * count, 2 * LANES), BF16)
    pieces = jnp.concatenate(three_parts(stacked) + (pad,), axis=0)
    terms[...] = jnp.dot(place_r, pieces, preferred_element_type=F32).reshape(terms.shape)

    def t_copy(src, at, to, sem):
        return pltpu.make_async_remote_copy(
            src_ref=terms.at[src],
            dst_ref=rt.at[at],
            send_sem=tsend.at[sem],
            recv_sem=trecv.at[at],
            device_id={"col": to},
            device_id_type=MESH,
        )

    def t_start(k):
        to = far_first(col, n_col, k)
        t_copy(to, col, to, k).start()

    each(n_col, t_start)
    rt[col] = terms[col]

    xn_out = pltpu.make_async_copy(xn_s.at[row], xn_o, lsem.at[12])
    xn_out.start()
    resid = jnp.where(
        kinds == 0,
        reduced,
        jnp.where(
            kinds == 1,
            jnp.minimum(reduced, 0.0),
            jnp.where(kinds == 2, jnp.maximum(reduced, 0.0), 0.0),
        ),
    )
    bounds = jnp.where(has_low, low * jnp.maximum(reduced, 0.0), 0.0) + jnp.where(
        has_up, high * jnp.minimum(reduced, 0.0), 0.0
    )
    y = ybuf[col]
    b = bbuf[...]
    dual_sum = 0.5 * total(resid * resid)
    gap = 0.5 * total(c * x_next - bounds) - total(b * y)
    lane1 = iota((1, LANES), 1)
    rows_total = ybuf.shape[1] * LANES * n_dev
    cols_total = cblocks * LANES * n_dev
    early_stats = jnp.where(
        lane1 == 1, dual_sum / cols_total, jnp.where(lane1 == 2, gap / math.sqrt(cols_total), 0.0)
    )
    ineq = ebuf[...] == 1

    def t_wait(k):
        t_copy(0, lax.rem(col + k, n_col), col, k).wait_recv()

    each(n_col, t_wait)
    totals = jnp.sum(rt[...], axis=0)
    y_next = y + step[1] * (b - totals[:, :LANES])
    yn_s[...] = jnp.where(ineq, jnp.maximum(y_next, 0.0), y_next)
    p_resid = b - totals[:, LANES:]
    p_resid = jnp.where(ineq, jnp.maximum(p_resid, 0.0), p_resid)
    sbuf[0] = jnp.where(lane1 == 0, total(p_resid * p_resid) / rows_total, early_stats)

    def s_copy(at, to, sem):
        return pltpu.make_async_remote_copy(
            src_ref=sbuf.at[0],
            dst_ref=stat_o.at[at],
            send_sem=ssend.at[sem],
            recv_sem=srecv.at[at],
            device_id={"col": lax.div(to, n_row), "row": lax.rem(to, n_row)},
            device_id_type=MESH,
        )

    each(n_dev, lambda k: s_copy(dev, far_first(dev, n_dev, k), k).start())
    own_stat = pltpu.make_async_copy(sbuf.at[0], stat_o.at[dev], lsem.at[18])
    own_stat.start()
    yn_out = pltpu.make_async_copy(yn_s, yn_o, lsem.at[13])
    yn_out.start()
    for copy in early:
        copy.wait_send()
    part_copy.wait_send()
    each(n_col, lambda k: y_copy(col, col, k).wait_send())
    each(n_col, lambda k: t_copy(0, col, col, k).wait_send())
    xn_out.wait()
    yn_out.wait()

    each(n_dev, lambda k: s_copy(lax.rem(dev + k, n_dev), dev, k).wait_recv())
    own_stat.wait()
    each(n_dev, lambda k: s_copy(dev, dev, k).wait_send())


def hand_on(x_i, y_i, stat_i, x_o, y_o, stat_o):
    x_o[...] = x_i[...]
    y_o[...] = y_i[...]
    stat_o[...] = jnp.sum(stat_i[...], axis=0)[0, :3]


def shards(
    tile_values,
    tile_blocks,
    scale_index,
    scale_table,
    primal_iter,
    dual_iter,
    objective,
    right_side,
    lower_bound,
    upper_bound,
    bound_kind,
    row_kind,
    step_sizes,
):
    n_col = lax.axis_size("col")
    n_row = lax.axis_size("row")
    n_dev = n_col * n_row
    count, size, _ = tile_values.shape
    cb = primal_iter.shape[1] // LANES
    rb = dual_iter.shape[1] // LANES
    wide = lambda a: a.reshape(-1, LANES)
    hbm = pl.BlockSpec(memory_space=pltpu.HBM)
    vmem = pl.BlockSpec(memory_space=pltpu.VMEM)
    dma = pltpu.SemaphoreType.DMA
    x_next, y_next, stats = pl.pallas_call(
        functools.partial(kernel, n_col, n_row),
        out_shape=(
            jax.ShapeDtypeStruct((cb, LANES), F32),
            jax.ShapeDtypeStruct((rb, LANES), F32),
            jax.ShapeDtypeStruct((n_dev, 1, LANES), F32),
        ),
        in_specs=[hbm] * 13,
        out_specs=(hbm, hbm, hbm),
        scratch_shapes=[
            pltpu.VMEM((count, size, size), BF16),
            pltpu.VMEM((count * size, size), BF16),
            pltpu.VMEM((4, n_row, cb, LANES), F32),
            pltpu.VMEM((n_row, cb, LANES), jnp.int32),
            pltpu.VMEM((n_col, rb, LANES), F32),
            pltpu.VMEM((rb, LANES), F32),
            pltpu.VMEM((rb, LANES), jnp.int32),
            pltpu.VMEM((n_row, 8, LANES), F32),
            pltpu.VMEM((n_row, 2, 32, LANES), F32),
            pltpu.VMEM((n_row, cb, LANES), F32),
            pltpu.VMEM((rb, LANES), F32),
            pltpu.VMEM((n_col, rb, 2 * LANES), F32),
            pltpu.VMEM((n_col, rb, 2 * LANES), F32),
            pltpu.VMEM((1, 1, LANES), F32),
            pltpu.SMEM((2, count), jnp.int32),
            pltpu.SMEM(scale_index.shape, jnp.int32),
            pltpu.SMEM(scale_table.shape, F32),
            pltpu.SMEM(step_sizes.shape, F32),
            dma((19,)),
            dma((n_col,)),
            dma((n_col,)),
            dma((7,)),
            dma((7,)),
            dma((n_col,)),
            dma((n_col,)),
            dma((n_dev,)),
            dma((n_dev,)),
        ],
        compiler_params=pltpu.CompilerParams(
            collective_id=0, has_side_effects=True, vmem_limit_bytes=64 * 1024 * 1024
        ),
    )(
        tile_values,
        tile_blocks.T,
        scale_index,
        scale_table,
        wide(primal_iter),
        wide(dual_iter),
        wide(objective),
        wide(right_side),
        wide(lower_bound),
        wide(upper_bound),
        wide(bound_kind),
        wide(row_kind),
        step_sizes,
    )
    x_next, y_next, stats = pl.pallas_call(
        hand_on,
        out_shape=(
            jax.ShapeDtypeStruct((cb, LANES), F32),
            jax.ShapeDtypeStruct((rb, LANES), F32),
            jax.ShapeDtypeStruct((3,), F32),
        ),
        in_specs=[vmem] * 3,
        out_specs=(vmem, vmem, vmem),
        scratch_shapes=[],
        compiler_params=pltpu.CompilerParams(vmem_limit_bytes=64 * 1024 * 1024),
    )(x_next, y_next, stats)
    return (x_next.reshape(1, -1), y_next.reshape(1, -1), stats)


def solution(mesh):
    return jax.shard_map(
        shards,
        mesh=mesh,
        in_specs=(
            P(("group", "col", "row"), None, None),
            P(("group", "col", "row"), None),
            P(("group", "col", "row")),
            P("group"),
            P(("group", "col"), "row"),
            P(("group", "row"), "col"),
            P(("group", "col"), "row"),
            P(("group", "row"), "col"),
            P(("group", "col"), "row"),
            P(("group", "col"), "row"),
            P(("group", "col"), "row"),
            P(("group", "row"), "col"),
            P("group"),
        ),
        out_specs=(P(("group", "col"), "row"), P(("group", "row"), "col"), P("group")),
        check_vma=False,
    )
```

```python
import functools
import math

import jax
import jax.numpy as jnp
from jax import lax
from jax.experimental import pallas as pl
from jax.experimental.pallas import tpu as pltpu
from jax.sharding import PartitionSpec as P

F32 = jnp.float32
BF16 = jnp.bfloat16
MESH = pl.DeviceIdType.MESH
LANES = 128


def each(count, body):
    if count <= 17:
        for k in range(1, count):
            body(k)
    else:
        lax.fori_loop(1, count, lambda k, _: (body(k), 0)[1], 0)


def three_parts(v):
    hi = v.astype(BF16)
    rest = v - hi.astype(F32)
    mid = rest.astype(BF16)
    low = (rest - mid.astype(F32)).astype(BF16)
    return hi, mid, low


def far_first(me, count, k):
    j = k - 1
    up = lax.div(2 * me, count)
    rising = j + lax.div(j + count - me, count)
    falling = count - 1 - j - lax.div(j + 1 + me, count)
    return up * rising + (1 - up) * falling


def total(v):
    return jnp.sum(jnp.sum(v, axis=0, keepdims=True), axis=1, keepdims=True)


def iota(shape, dim):
    return lax.broadcasted_iota(jnp.int32, shape, dim)


def kernel(
    n_col,
    n_row,
    tv, tb_h, si_h, st_h, x_h, y_h, c_h, b_h, l_h, u_h, k_h, e_h, step_h,
    xn_o, yn_o, stat_o,
    tiles, flipped, prim, kind, ybuf, bbuf, ebuf, meta, part, xn_s, yn_s, terms, rt, sbuf,
    tb, si, st, step, lsem, ysend, yrecv, rsend, rrecv, tsend, trecv, ssend, srecv,
):
    count, size, _ = tv.shape
    groups = count // 8
    cblocks = prim.shape[2]
    n_dev = n_col * n_row
    col = lax.axis_index("col")
    row = lax.axis_index("row")
    other = 1 - row
    dev = col * n_row + row
    row_span = ybuf.shape[1] // 2 * n_col
    col_span = cblocks

    barrier = pltpu.get_barrier_semaphore()

    def greet(k):
        q = far_first(dev, n_dev, k)
        pl.semaphore_signal(
            barrier,
            inc=1,
            device_id={"col": lax.div(q, n_row), "row": lax.rem(q, n_row)},
            device_id_type=MESH,
        )

    each(n_dev, greet)

    y_in = pltpu.make_async_copy(y_h, ybuf.at[col], lsem.at[0])
    y_in.start()
    scalar_in = [
        pltpu.make_async_copy(src, dst, lsem.at[14 + i])
        for i, (src, dst) in enumerate(((tb_h, tb), (si_h, si), (st_h, st), (step_h, step)))
    ]
    for copy in scalar_in:
        copy.start()
    chunk = count // 4
    tile_in = []
    for i in range(4):
        span = pl.ds(i * chunk, chunk)
        copy = pltpu.make_async_copy(tv.at[span], tiles.at[span], lsem.at[1 + i])
        copy.start()
        tile_in.append(copy)
    small_in = [
        pltpu.make_async_copy(src, prim.at[i, row], lsem.at[5 + i])
        for i, src in enumerate((x_h, c_h, l_h, u_h))
    ]
    small_in.append(pltpu.make_async_copy(k_h, kind.at[row], lsem.at[9]))
    small_in.append(pltpu.make_async_copy(b_h, bbuf, lsem.at[10]))
    small_in.append(pltpu.make_async_copy(e_h, ebuf, lsem.at[11]))
    for copy in small_in:
        copy.start()

    for copy in scalar_in:
        copy.wait()
    sub8 = iota((8, LANES), 0)
    lane8 = iota((8, LANES), 1)
    lane256 = iota((8, 2 * LANES), 1)
    rows_l = [tb[0, s] - row * row_span for s in range(count)]
    cols_l = [tb[1, s] - col * col_span for s in range(count)]
    own = lane8 // 64 == row
    spot = lane8 % 64
    mine = jnp.where(own, -1.0, 0.0)
    for s in range(count):
        at = (2 * cols_l[s]).astype(F32)
        mine = jnp.where(own & (spot == s), at, mine)
        mine = jnp.where(own & (spot == 32 + s), at + 1.0, mine)
    meta[row] = mine

    y_in.wait()
    pl.semaphore_wait(barrier, n_dev - 1)

    def y_copy(at, to, sem):
        return pltpu.make_async_remote_copy(
            src_ref=ybuf.at[col],
            dst_ref=ybuf.at[at],
            send_sem=ysend.at[sem],
            recv_sem=yrecv.at[at],
            device_id={"col": to},
            device_id_type=MESH,
        )

    each(n_col, lambda k: y_copy(col, far_first(col, n_col, k), k).start())

    def row_copy(src, dst, i):
        return pltpu.make_async_remote_copy(
            src_ref=src,
            dst_ref=dst,
            send_sem=rsend.at[i],
            recv_sem=rrecv.at[i],
            device_id={"row": other},
            device_id_type=MESH,
        )

    early = [row_copy(src, prim.at[i, row], i) for i, src in enumerate((x_h, c_h, l_h, u_h))]
    early.append(row_copy(k_h, kind.at[row], 4))
    early.append(row_copy(meta.at[row], meta.at[row], 5))
    for copy in early:
        copy.start()

    scales = [st[si[s]] for s in range(count)]
    scale8, row8, col8 = [], [], []
    for g in range(groups):
        sc = jnp.zeros((8, LANES), F32)
        rr = jnp.zeros((8, LANES), jnp.int32)
        cc = jnp.zeros((8, LANES), jnp.int32)
        for t in range(8):
            s = g * 8 + t
            sc = jnp.where(sub8 == t, scales[s], sc)
            rr = jnp.where(sub8 == t, 2 * rows_l[s], rr)
            cc = jnp.where(sub8 == t, 2 * cols_l[s], cc)
        scale8.append(jnp.concatenate([sc, sc], axis=1))
        row8.append(rr)
        col8.append(cc)

    wide_rows = ybuf.shape[1] * n_col
    tgt_y = jnp.concatenate(row8 + [jnp.full((8, LANES), -2, jnp.int32)], axis=0)
    reps = max(1, wide_rows // LANES)
    if wide_rows < LANES:
        tgt_y = tgt_y[:, :wide_rows]
    else:
        tgt_y = jnp.concatenate([tgt_y] * reps, axis=1)
    lane_y = iota(tgt_y.shape, 1)
    pick_y = [(lane_y == tgt_y + h).astype(F32).astype(BF16) for h in range(2)]

    tgt_p = jnp.concatenate([v for cc in col8 for v in (cc, cc + 2 * col_span)], axis=0)
    reps = 4 * col_span // LANES
    tgt_p = jnp.concatenate([tgt_p] * reps, axis=1)
    lane_p = iota(tgt_p.shape, 1)
    pick_p = [(lane_p == tgt_p + h).astype(F32).astype(BF16) for h in range(2)]

    spot3 = lane256 % (2 * count)
    live = lane256 < 6 * count
    tgt_r = jnp.full((8, 2 * LANES), -1, jnp.int32)
    for s in range(count):
        tgt_r = jnp.where(live & (spot3 == s), 2 * rows_l[s], tgt_r)
        tgt_r = jnp.where(live & (spot3 == count + s), 2 * rows_l[s] + 1, tgt_r)
    place_r = (iota((wide_rows, 2 * LANES), 0) == tgt_r[0:1]).astype(F32).astype(BF16)

    for i, copy in enumerate(tile_in):
        copy.wait()
        for s in range(i * chunk, (i + 1) * chunk):
            flipped[s * size : (s + 1) * size] = tiles[s].T
    each(n_col, lambda k: y_copy(lax.rem(col + k, n_col), col, k).wait_recv())

    y_b = ybuf[...].reshape(wide_rows, LANES).astype(BF16)
    y_pick = jnp.concatenate(
        [jnp.dot(pick, y_b, preferred_element_type=F32) for pick in pick_y], axis=1
    )
    sub_y = iota((8, size), 0)
    product = []
    for g in range(groups):
        rows8 = y_pick[8 * g : 8 * g + 8]
        lhs = jnp.concatenate(
            [jnp.where(sub_y == t, rows8, 0.0) for t in range(8)], axis=1
        ).astype(BF16)
        weights = tiles[8 * g : 8 * g + 8].reshape(8 * size, size)
        product.append(jnp.dot(lhs, weights, preferred_element_type=F32) * scale8[g])
    product = jnp.concatenate(product + [jnp.zeros((8, size), F32)], axis=0)
    part[row, 0] = product[:, :LANES]
    part[row, 1] = product[:, LANES:]
    part_copy = row_copy(part.at[row], part.at[row], 6)
    part_copy.start()

    for copy in small_in:
        copy.wait()
    late = [row_copy(x_h, prim.at[i, other], i) for i in range(4)]
    late.append(row_copy(k_h, kind.at[other], 4))
    late.append(row_copy(meta.at[row], meta.at[other], 5))
    for copy in late:
        copy.wait_recv()
    targets = (meta[0] + meta[1])[0:1]
    place_c = (iota((2 * col_span, LANES), 0).astype(F32) == targets).astype(F32).astype(BF16)
    place_c = jnp.concatenate([place_c] * 3, axis=1)

    row_copy(part.at[row], part.at[other], 6).wait_recv()
    pieces = jnp.concatenate(three_parts(part[...].reshape(LANES, LANES)), axis=0)
    aty = jnp.dot(place_c, pieces, preferred_element_type=F32)

    full = (2 * cblocks, LANES)
    x, c, low, high = [prim[i].reshape(full) for i in range(4)]
    kinds = kind[...].reshape(full)
    reduced = c - aty
    has_low = (kinds == 1) | (kinds == 3)
    has_up = (kinds == 2) | (kinds == 3)
    moved = x - step[0] * reduced
    moved = jnp.where(has_low, jnp.maximum(moved, low), moved)
    x_next = jnp.where(has_up, jnp.minimum(moved, high), moved)
    xn_s[...] = x_next.reshape(xn_s.shape)
    pair = jnp.concatenate([2.0 * x_next - x, x_next], axis=0).astype(BF16)

    p_pick = jnp.concatenate(
        [jnp.dot(pick, pair, preferred_element_type=F32) for pick in pick_p], axis=1
    )
    sub_p = iota((16, size), 0) % 8
    bars, news = [], []
    for g in range(groups):
        rows16 = p_pick[16 * g : 16 * g + 16]
        lhs = jnp.concatenate(
            [jnp.where(sub_p == t, rows16, 0.0).astype(BF16) for t in range(8)], axis=1
        )
        weights = flipped[8 * g * size : 8 * (g + 1) * size]
        acc = jnp.dot(lhs, weights, preferred_element_type=F32)
        bars.append(acc[:8] * scale8[g])
        news.append(acc[8:] * scale8[g])
    bar = jnp.concatenate(bars, axis=0)
    new = jnp.concatenate(news, axis=0)
    stacked = jnp.concatenate(
        [
            jnp.concatenate([bar[:, :LANES], new[:, :LANES]], axis=1),
            jnp.concatenate([bar[:, LANES:], new[:, LANES:]], axis=1),
        ],
        axis=0,
    )
    pad = jnp.zeros((2 * LANES - 6 * count, 2 * LANES), BF16)
    pieces = jnp.concatenate(three_parts(stacked) + (pad,), axis=0)
    terms[...] = jnp.dot(place_r, pieces, preferred_element_type=F32).reshape(terms.shape)

    def t_copy(src, at, to, sem):
        return pltpu.make_async_remote_copy(
            src_ref=terms.at[src],
            dst_ref=rt.at[at],
            send_sem=tsend.at[sem],
            recv_sem=trecv.at[at],
            device_id={"col": to},
            device_id_type=MESH,
        )

    def t_start(k):
        to = far_first(col, n_col, k)
        t_copy(to, col, to, k).start()

    each(n_col, t_start)
    rt[col] = terms[col]

    xn_out = pltpu.make_async_copy(xn_s.at[row], xn_o, lsem.at[12])
    xn_out.start()
    resid = jnp.where(
        kinds == 0,
        reduced,
        jnp.where(
            kinds == 1,
            jnp.minimum(reduced, 0.0),
            jnp.where(kinds == 2, jnp.maximum(reduced, 0.0), 0.0),
        ),
    )
    bounds = jnp.where(has_low, low * jnp.maximum(reduced, 0.0), 0.0) + jnp.where(
        has_up, high * jnp.minimum(reduced, 0.0), 0.0
    )
    y = ybuf[col]
    b = bbuf[...]
    dual_sum = 0.5 * total(resid * resid)
    gap = 0.5 * total(c * x_next - bounds) - total(b * y)
    lane1 = iota((1, LANES), 1)
    rows_total = ybuf.shape[1] * LANES * n_dev
    cols_total = cblocks * LANES * n_dev
    early_stats = jnp.where(
        lane1 == 1, dual_sum / cols_total, jnp.where(lane1 == 2, gap / math.sqrt(cols_total), 0.0)
    )
    ineq = ebuf[...] == 1

    def t_wait(k):
        t_copy(0, lax.rem(col + k, n_col), col, k).wait_recv()

    each(n_col, t_wait)
    totals = jnp.sum(rt[...], axis=0)
    y_next = y + step[1] * (b - totals[:, :LANES])
    yn_s[...] = jnp.where(ineq, jnp.maximum(y_next, 0.0), y_next)
    p_resid = b - totals[:, LANES:]
    p_resid = jnp.where(ineq, jnp.maximum(p_resid, 0.0), p_resid)
    sbuf[0] = jnp.where(lane1 == 0, total(p_resid * p_resid) / rows_total, early_stats)

    def s_copy(at, to, sem):
        return pltpu.make_async_remote_copy(
            src_ref=sbuf.at[0],
            dst_ref=stat_o.at[at],
            send_sem=ssend.at[sem],
            recv_sem=srecv.at[at],
            device_id={"col": lax.div(to, n_row), "row": lax.rem(to, n_row)},
            device_id_type=MESH,
        )

    each(n_dev, lambda k: s_copy(dev, far_first(dev, n_dev, k), k).start())
    own_stat = pltpu.make_async_copy(sbuf.at[0], stat_o.at[dev], lsem.at[18])
    own_stat.start()
    yn_out = pltpu.make_async_copy(yn_s, yn_o, lsem.at[13])
    yn_out.start()
    xn_out.wait()
    yn_out.wait()

    each(n_dev, lambda k: s_copy(lax.rem(dev + k, n_dev), dev, k).wait_recv())
    own_stat.wait()
    for copy in early:
        copy.wait_send()
    part_copy.wait_send()
    each(n_col, lambda k: y_copy(col, col, k).wait_send())
    each(n_col, lambda k: t_copy(0, col, col, k).wait_send())
    each(n_dev, lambda k: s_copy(dev, dev, k).wait_send())


def hand_on(x_i, y_i, stat_i, x_o, y_o, stat_o):
    x_o[...] = x_i[...]
    y_o[...] = y_i[...]
    stat_o[...] = jnp.sum(stat_i[...], axis=0)[0, :3]


def shards(
    tile_values,
    tile_blocks,
    scale_index,
    scale_table,
    primal_iter,
    dual_iter,
    objective,
    right_side,
    lower_bound,
    upper_bound,
    bound_kind,
    row_kind,
    step_sizes,
):
    n_col = lax.axis_size("col")
    n_row = lax.axis_size("row")
    n_dev = n_col * n_row
    count, size, _ = tile_values.shape
    cb = primal_iter.shape[1] // LANES
    rb = dual_iter.shape[1] // LANES
    wide = lambda a: a.reshape(-1, LANES)
    hbm = pl.BlockSpec(memory_space=pltpu.HBM)
    vmem = pl.BlockSpec(memory_space=pltpu.VMEM)
    dma = pltpu.SemaphoreType.DMA
    x_next, y_next, stats = pl.pallas_call(
        functools.partial(kernel, n_col, n_row),
        out_shape=(
            jax.ShapeDtypeStruct((cb, LANES), F32),
            jax.ShapeDtypeStruct((rb, LANES), F32),
            jax.ShapeDtypeStruct((n_dev, 1, LANES), F32),
        ),
        in_specs=[hbm] * 13,
        out_specs=(hbm, hbm, hbm),
        scratch_shapes=[
            pltpu.VMEM((count, size, size), BF16),
            pltpu.VMEM((count * size, size), BF16),
            pltpu.VMEM((4, n_row, cb, LANES), F32),
            pltpu.VMEM((n_row, cb, LANES), jnp.int32),
            pltpu.VMEM((n_col, rb, LANES), F32),
            pltpu.VMEM((rb, LANES), F32),
            pltpu.VMEM((rb, LANES), jnp.int32),
            pltpu.VMEM((n_row, 8, LANES), F32),
            pltpu.VMEM((n_row, 2, 32, LANES), F32),
            pltpu.VMEM((n_row, cb, LANES), F32),
            pltpu.VMEM((rb, LANES), F32),
            pltpu.VMEM((n_col, rb, 2 * LANES), F32),
            pltpu.VMEM((n_col, rb, 2 * LANES), F32),
            pltpu.VMEM((1, 1, LANES), F32),
            pltpu.SMEM((2, count), jnp.int32),
            pltpu.SMEM(scale_index.shape, jnp.int32),
            pltpu.SMEM(scale_table.shape, F32),
            pltpu.SMEM(step_sizes.shape, F32),
            dma((19,)),
            dma((n_col,)),
            dma((n_col,)),
            dma((7,)),
            dma((7,)),
            dma((n_col,)),
            dma((n_col,)),
            dma((n_dev,)),
            dma((n_dev,)),
        ],
        compiler_params=pltpu.CompilerParams(
            collective_id=0, has_side_effects=True, vmem_limit_bytes=64 * 1024 * 1024
        ),
    )(
        tile_values,
        tile_blocks.T,
        scale_index,
        scale_table,
        wide(primal_iter),
        wide(dual_iter),
        wide(objective),
        wide(right_side),
        wide(lower_bound),
        wide(upper_bound),
        wide(bound_kind),
        wide(row_kind),
        step_sizes,
    )
    x_next, y_next, stats = pl.pallas_call(
        hand_on,
        out_shape=(
            jax.ShapeDtypeStruct((cb, LANES), F32),
            jax.ShapeDtypeStruct((rb, LANES), F32),
            jax.ShapeDtypeStruct((3,), F32),
        ),
        in_specs=[vmem] * 3,
        out_specs=(vmem, vmem, vmem),
        scratch_shapes=[],
        compiler_params=pltpu.CompilerParams(vmem_limit_bytes=64 * 1024 * 1024),
    )(x_next, y_next, stats)
    return (x_next.reshape(1, -1), y_next.reshape(1, -1), stats)


def solution(mesh):
    return jax.shard_map(
        shards,
        mesh=mesh,
        in_specs=(
            P(("group", "col", "row"), None, None),
            P(("group", "col", "row"), None),
            P(("group", "col", "row")),
            P("group"),
            P(("group", "col"), "row"),
            P(("group", "row"), "col"),
            P(("group", "col"), "row"),
            P(("group", "row"), "col"),
            P(("group", "col"), "row"),
            P(("group", "col"), "row"),
            P(("group", "col"), "row"),
            P(("group", "row"), "col"),
            P("group"),
        ),
        out_specs=(P(("group", "col"), "row"), P(("group", "row"), "col"), P("group")),
        check_vma=False,
    )
```
